512 devices in a mesh: seg: 32 (over x, y_lo, core), video: 16 (over y_hi, z).
Axes of the slice: x: 4, y: 8 (y_hi: 2, y_lo: 4; y = y_hi * 4 + y_lo), z: 8, core: 2. Of those that a mesh axis runs over, the one named last changes fastest.
Arguments:
- tokens: bfloat16 [2, 2048, 3072], P(None, 'seg'), may hold values from -6 to 6
- prompt_ids: int32 [2, 32], P(None, 'seg'), may hold values from 0 to 15
- prompt_table: bfloat16 [16, 3072], replicated, may hold values from -6 to 6
- qkv_weight: bfloat16 [3072, 3, 2048], P('seg', None, 'video'), may hold values from -0.109375 to 0.109375
- out_weight: bfloat16 [2048, 3072], P('seg', 'video'), may hold values from -0.125 to 0.125
- init_first: bfloat16 [32, 64, 256], P('video'), may hold values from -0.75 to 0.75
- init_second: bfloat16 [32, 64, 256], P('video'), may hold values from -0.375 to 0.375
- inner_rate: float32 [32], P('video'), may hold values from 0.002 to 0.02
Outputs:
- mixed: bfloat16 [2, 2048, 3072], P(None, 'seg', 'video')
The draws below stay inside these ranges and needn't reach their ends.
All inputs are finite; a program needn't handle non-finite values.
Results may differ from the reference program's by a relative error of at most 0.01.
Values may be sent and summed in bfloat16 or wider, within the bound.
A program may use at most 64 MiB of HBM per device.

```python
import math
import jax
import jax.numpy as jnp
from jax import lax

D = 3072
HS = 64
INNER = 256
H = 32
TOK_DEV = 64
VIDEOS = 2
PROMPTS = 16
TOKENS = 2048
N_SEG = 32


def set_ends(drawn, stream_key, least, high):
    extent = drawn.shape
    place = [jax.random.randint(jax.random.fold_in(stream_key, axis), (), 0, extent[axis]) for axis in range(len(extent))]
    drawn = drawn.at[tuple(place)].set(least)
    longest = extent.index(max(extent))
    place[longest] = (place[longest] + 1) % extent[longest]
    return drawn.at[tuple(place)].set(high)


def steps_of(rng, dims, pieces, smallest, largest):
    def one(position, shards_of):
        heights = jax.random.uniform(jax.random.fold_in(jax.random.fold_in(rng, 6), position), (shards_of,), jnp.float32, smallest / len(pieces), largest / len(pieces))
        return jnp.repeat(jnp.exp(heights), dims[position] // shards_of).reshape((-1,) + (1,) * (len(dims) - position - 1))

    level = one(*pieces[0])
    for cut in pieces[1:]:
        level = level * one(*cut)
    return level


def gaussian(stream_key, dims, deviation, reach, split=(), held_as=jnp.bfloat16):
    values = deviation * jax.random.normal(stream_key, dims, jnp.float32)
    if split:
        values = values * steps_of(stream_key, dims, split, -0.22, 0.18)
    return jnp.clip(values, -reach, reach).astype(held_as)


def setup_inputs(seed: int = 0) -> dict:
    key_of = jax.random.split(jax.random.key(seed), 9)
    return {
        "tokens": gaussian(key_of[0], (VIDEOS, TOKENS, D), 1.0, 6.0, ((1, 32),)),
        "prompt_ids": set_ends(jax.random.randint(key_of[1], (VIDEOS, N_SEG), 0, PROMPTS), jax.random.fold_in(key_of[1], 1), 0, PROMPTS - 1).astype(jnp.int32),
        "prompt_table": gaussian(key_of[2], (PROMPTS, D), 1.0, 6.0),
        "qkv_weight": gaussian(key_of[3], (D, 3, H * HS), D ** -0.5, 0.109375, ((0, 32), (2, 16))),
        "out_weight": gaussian(key_of[4], (H * HS, D), (H * HS) ** -0.5, 0.125, ((0, 32), (1, 16))),
        "init_first": gaussian(key_of[5], (H, HS, INNER), HS ** -0.5, 0.75, ((0, 16),)),
        "init_second": gaussian(key_of[6], (H, HS, INNER), INNER ** -0.5, 0.375, ((0, 16),)),
        "inner_rate": jnp.clip(jnp.exp(math.log(0.02) - 2.30258502 * jax.random.uniform(key_of[7], (H,), jnp.float32) ** steps_of(key_of[7], (H,), ((0, 16),), -0.2, 0.2)), 0.002, 0.02),
    }


HIGH = lax.Precision.HIGHEST

def inner_apply(first_layer, second_layer, inputs):
    pre_act = jnp.einsum('ms,si->mi', inputs, first_layer, precision=HIGH)
    hidden = jax.nn.gelu(pre_act, approximate=True)
    result = jnp.einsum('mi,si->ms', hidden, second_layer, precision=HIGH)
    centred = result - lax.optimization_barrier(jnp.mean(result, -1, keepdims=True))
    spread = lax.optimization_barrier(jnp.mean(centred * centred, -1, keepdims=True))
    return centred * lax.rsqrt(spread + 1e-06)

def inner_loss(first_layer, second_layer, keys_block, values_block):
    differ = inner_apply(first_layer, second_layer, keys_block) - (values_block - keys_block)
    return 0.5 * jnp.sum(differ * differ) / keys_block.shape[0]

def inner_step(first_layer, second_layer, rate, query_block, keys_block, values_block):
    grad_first, grad_second = jax.grad(inner_loss, argnums=(0, 1))(first_layer, second_layer, keys_block, values_block)
    first_layer = first_layer - rate * grad_first
    second_layer = second_layer - rate * grad_second
    return (first_layer, second_layer, query_block + inner_apply(first_layer, second_layer, query_block))

def settle(weights):
    return lax.optimization_barrier(weights.astype(jnp.bfloat16)).astype(jnp.float32)

def one_chain(first_layer, second_layer, rate, queries, keys_all, values_all):

    def segment(carry, block):
        layer_one, layer_two = carry
        query_seg, key_seg, value_seg = block
        results = []
        for minibatch in range(4):
            layer_one, layer_two, answer = inner_step(layer_one, layer_two, rate, query_seg[minibatch], key_seg[minibatch], value_seg[minibatch])
            results.append(answer)
        return ((settle(layer_one), settle(layer_two)), jnp.stack(results))
    _, answers = lax.scan(segment, (first_layer, second_layer), (queries, keys_all, values_all))
    return answers

def reference(tokens, prompt_ids, prompt_table, qkv_weight, out_weight, init_first, init_second, inner_rate):
    onehot = (prompt_ids[:, :, None] == jnp.arange(PROMPTS, dtype=jnp.int32)).astype(jnp.float32)
    prompt_bias = jnp.einsum('vsp,pd->vsd', onehot, prompt_table.astype(jnp.float32))
    prompt_bias = jnp.repeat(prompt_bias, TOK_DEV, axis=1)
    xin = (tokens.astype(jnp.float32) + prompt_bias).astype(jnp.bfloat16)
    qkv = jnp.dot(xin.reshape(VIDEOS * TOKENS, D), qkv_weight.reshape(D, 3 * H * HS), preferred_element_type=jnp.float32).astype(jnp.bfloat16)
    parts = qkv.astype(jnp.float32).reshape(VIDEOS, N_SEG, 4, TOK_DEV // 4, 3, H, HS)
    parts = jnp.transpose(parts, (4, 0, 5, 1, 2, 3, 6))
    queries, keys_all, values_all = (parts[0], parts[1], parts[2])
    layer_one = init_first.astype(jnp.float32)
    layer_two = init_second.astype(jnp.float32)
    per_head = jax.vmap(one_chain, in_axes=(0, 0, 0, 0, 0, 0))
    per_video = jax.vmap(per_head, in_axes=(None, None, None, 0, 0, 0))
    forward = per_video(layer_one, layer_two, inner_rate, queries, keys_all, values_all)
    backward = per_video(layer_one, layer_two, inner_rate, queries[:, :, ::-1, ::-1], keys_all[:, :, ::-1, ::-1], values_all[:, :, ::-1, ::-1])
    backward = backward[:, :, ::-1, ::-1]
    heads = (forward + backward).astype(jnp.bfloat16)
    heads = jnp.transpose(heads, (0, 2, 3, 4, 1, 5)).reshape(VIDEOS * TOKENS, H * HS)
    mixed = jnp.dot(heads, out_weight, preferred_element_type=jnp.float32).astype(jnp.bfloat16)
    return mixed.reshape(VIDEOS, TOKENS, D)
```

```python
import jax
import jax.numpy as jnp
from jax import lax
from jax.experimental import pallas as pl
from jax.experimental.pallas import tpu as pltpu
from jax.sharding import PartitionSpec as P

HS = 64
MINI = 16
SEGS = 32
GROUPS = 16
VIDEOS = 2
ROWS = 64
EPS = 1e-6
C0 = 0.7978845608028654
C1 = C0 * 0.044715
f32 = jnp.float32
bf16 = jnp.bfloat16


def contract(a, b, da, db):
    return lax.dot_general(a, b, (((da,), (db,)), ((), ())), preferred_element_type=f32)


def nn(a, b):
    return contract(a, b, 1, 0)


def nt(a, b):
    return contract(a, b, 1, 1)


def tn(a, b):
    return contract(a, b, 0, 0)


def gelu_parts(x):
    x2 = x * x
    t = jnp.tanh(x * (C0 + C1 * x2))
    half = 0.5 * x
    return half + half * t, t, x2, half


def gelu_slope(t, x2, half):
    return (0.5 + 0.5 * t) + half * (1.0 - t * t) * (C0 + (3.0 * C1) * x2)


def remote(src, dst, send, recv, seg=None, video=None):
    where = {"seg": seg} if video is None else {"video": video}
    return pltpu.make_async_remote_copy(
        src_ref=src,
        dst_ref=dst,
        send_sem=send,
        recv_sem=recv,
        device_id=where,
        device_id_type=pl.DeviceIdType.MESH,
    )


def landed(ref, sem):
    pltpu.make_async_copy(ref, ref, sem).wait()


def kernel(
    rate_ref,
    ids_ref,
    tok_ref,
    table_ref,
    w_ref,
    ow_ref,
    first_ref,
    second_ref,
    out_ref,
    tok,
    xin,
    wall,
    acc,
    qmsg,
    qin,
    zst,
    zbuf,
    owall,
    heads,
    first,
    second,
    load_sem,
    w_send,
    w_recv,
    y_send,
    q_send,
    q_recv,
    o_send,
    o_recv,
    z_send,
    z_recv,
    h_send,
    h_recv,
):
    me = lax.axis_index("seg")
    vid = lax.axis_index("video")
    core = me % 2
    chip = me // 2
    x = chip // 4
    y = chip % 4

    def at(xx, yy, cc):
        return ((xx % 4) * 4 + yy) * 2 + cc

    load = pltpu.make_async_copy(tok_ref, tok, load_sem)
    load.start()

    barrier = pltpu.get_barrier_semaphore()

    def greet_seg(i, carry):
        pl.semaphore_signal(
            barrier, inc=1, device_id={"seg": (me + i) % SEGS}, device_id_type=pl.DeviceIdType.MESH
        )
        return carry

    def greet_video(i, carry):
        pl.semaphore_signal(
            barrier, inc=1, device_id={"video": (vid + i) % GROUPS}, device_id_type=pl.DeviceIdType.MESH
        )
        return carry

    lax.fori_loop(1, SEGS, greet_seg, 0)
    lax.fori_loop(1, GROUPS, greet_video, 0)
    pl.semaphore_wait(barrier, SEGS - 1 + GROUPS - 1)

    right, left, mate = at(x + 1, y, core), at(x + 3, y, core), at(x, y, 1 - core)
    y1 = y + 1 - 2 * (y % 2)
    y2 = (y + 2) % 4
    y3 = 3 - y

    def y_of(k):
        return jnp.where(k == 0, y, jnp.where(k == 1, y1, jnp.where(k == 2, y2, y3)))

    def pass_on(chunk, which, target, src=None):
        remote(
            wall.at[chunk] if src is None else src,
            wall.at[chunk],
            w_send.at[chunk, which],
            w_recv.at[chunk],
            seg=target,
        ).start()

    for k, yy in enumerate((y1, y2, y3)):
        remote(w_ref, wall.at[me], y_send.at[k], w_recv.at[me], seg=at(x, yy, core)).start()
    pass_on(me, 0, right, w_ref)
    pass_on(me, 1, left, w_ref)
    pass_on(me, 2, mate, w_ref)
    wall[me] = w_ref[...]

    load.wait()
    lane = lax.broadcasted_iota(jnp.int32, (16, 16), 1)
    picks = [jnp.where(lane == ids_ref[v, 0], 1.0, 0.0).astype(bf16) for v in range(VIDEOS)]

    def prepare(g, carry):
        span = pl.ds(pl.multiple_of(g * 384, 128), 384)
        for v in range(VIDEOS):
            bias = nn(picks[v], table_ref[:, span])[0:1]
            part = (tok[v, :, span].astype(f32) + bias).astype(bf16)
            for i in range(4):
                xin[g * 4 + i, ROWS * v : ROWS * (v + 1), 0:96] = part[:, 96 * i : 96 * (i + 1)]
        return carry

    def y_step(k, carry):
        chunk = at(x, y_of(k), core)
        landed(wall.at[chunk], w_recv.at[chunk])
        pass_on(chunk, 0, right)
        pass_on(chunk, 1, left)
        pass_on(chunk, 2, mate)
        return carry

    def add(chunk):
        acc[...] += nn(xin[chunk, :, 0:96], wall[chunk])

    lax.fori_loop(0, 8, prepare, 0)
    lax.fori_loop(1, 4, y_step, 0)
    acc[...] = jnp.zeros_like(acc)

    def x_step(k, carry):
        row = y_of(k)
        a = at(x + 3, row, core)
        b = at(x + 1, row, core)
        landed(wall.at[a], w_recv.at[a])
        pass_on(a, 2, mate)

        @pl.when(row < 2)
        def _():
            pass_on(a, 0, right)

        landed(wall.at[b], w_recv.at[b])
        pass_on(b, 2, mate)

        @pl.when(row >= 2)
        def _():
            pass_on(b, 1, left)

        add(at(x, row, core))
        add(a)
        add(b)
        c = at(x, row, 1 - core)
        landed(wall.at[c], w_recv.at[c])
        add(c)
        return carry

    lax.fori_loop(0, 4, x_step, 0)

    def far_step(k, carry):
        row = y_of(k)
        a = at(x + 2, row, core)
        landed(wall.at[a], w_recv.at[a])
        pass_on(a, 2, mate)
        add(a)
        for i in (1, 3):
            c = at(x + i, row, 1 - core)
            landed(wall.at[c], w_recv.at[c])
            add(c)
        return carry

    lax.fori_loop(0, 4, far_step, 0)

    def last_step(k, carry):
        c = at(x + 2, y_of(k), 1 - core)
        landed(wall.at[c], w_recv.at[c])
        add(c)
        return carry

    lax.fori_loop(0, 4, last_step, 0)

    for j in range(3):
        part = acc[:, 128 * j : 128 * (j + 1)]
        turned = pltpu.roll(part, 64, 1)
        for v in range(VIDEOS):
            qmsg[2 * v, j] = part[ROWS * v : ROWS * (v + 1)].astype(bf16)
            qmsg[2 * v + 1, j] = turned[ROWS * v : ROWS * (v + 1)].astype(bf16)

    def owner_of(i):
        return jnp.where(i < 4, i, SEGS - 8 + i)

    def give(i, carry):
        owner = owner_of(i)

        @pl.when(owner == me)
        def _():
            pltpu.make_async_copy(qmsg.at[i % 4], qin.at[me], q_recv.at[me]).start()

        @pl.when(owner != me)
        def _():
            remote(qmsg.at[i % 4], qin.at[me], q_send.at[i], q_recv.at[me], seg=owner).start()

        return carry

    lax.fori_loop(0, 8, give, 0)

    def give_out_weight(i):
        target = (me + i) % SEGS
        here = pl.ds(pl.multiple_of(me * 64, 64), 64)
        remote(ow_ref, owall.at[here], o_send.at[i], o_recv.at[me], seg=target).start()

    owall[pl.ds(pl.multiple_of(me * 64, 64), 64)] = ow_ref[...]

    is_owner = jnp.logical_or(me < 4, me >= SEGS - 4)
    back = jnp.where(me < 4, 0, 1)
    slot = jnp.where(me < 4, me, me - (SEGS - 8))
    head = me % 2

    def seg_of(j):
        return j + back * (SEGS - 1 - 2 * j)

    def give_answers(j):
        target = seg_of(j)

        @pl.when(target == me)
        def _():
            pltpu.make_async_copy(zst.at[target], zbuf.at[slot], z_recv.at[slot]).start()

        @pl.when(target != me)
        def _():
            remote(zst.at[target], zbuf.at[slot], z_send.at[target], z_recv.at[slot], seg=target).start()

    @pl.when(is_owner)
    def _():
        eta = rate_ref[head]
        first[...] = first_ref[head]
        second[...] = second_ref[head]
        offs = [pl.multiple_of(MINI * (t + back * (3 - 2 * t)), MINI) for t in range(4)]

        def segment(j, qprev):
            s = seg_of(j)
            before = jnp.where(j == 0, SEGS, seg_of(j - 1))
            landed(qin.at[s], q_recv.at[s])
            qs = [qin[s, 0, pl.ds(offs[t], MINI), 0:HS] for t in range(4)]
            ks = [qin[s, 1, pl.ds(offs[t], MINI), 0:HS] for t in range(4)]
            vs = [qin[s, 2, pl.ds(offs[t], MINI), 0:HS] for t in range(4)]
            keys = jnp.concatenate(ks, 0)
            both = jnp.concatenate([qprev, ks[0], qs[0], ks[1], qs[1], ks[2], qs[2], ks[3]], 0)
            layer_one = first[...]
            layer_two = second[...].astype(f32)
            mu = jnp.mean(layer_two, 0, keepdims=True)
            centred = layer_two - mu
            pre_all = nn(both, layer_one)
            cross = (-eta * nt(both, keys)).astype(bf16)
            pres = [pre_all[32 * t : 32 * t + 32] for t in range(4)]
            grads = []
            for t in range(4):
                target = vs[t].astype(f32) - ks[t].astype(f32)
                target = target - jnp.mean(target, -1, keepdims=True)
                h, th, x2, half = gelu_parts(pres[t])
                hb = h.astype(bf16)
                weights = centred.astype(bf16)
                c = nt(hb, weights)
                w = nn(target.astype(bf16), weights)
                ck = c[MINI:]
                u = nn(ck.astype(bf16), weights)
                rho = lax.rsqrt(jnp.mean(c * c, -1, keepdims=True) + EPS)
                m = jnp.mean(target * ck, -1, keepdims=True)
                rk = rho[MINI:]
                r2 = rk * rk
                b = rk * (1.0 / MINI)
                a = (r2 * (1.0 / MINI)) * (EPS * r2 + rk * m)
                slope = gelu_slope(th[MINI:], x2[MINI:], half[MINI:])
                grad = ((a * u - b * w) * slope).astype(bf16)
                grads.append(grad)
                for r in range(t + 1, 4):
                    pres[r] = pres[r] + nn(cross[32 * r : 32 * r + 32, MINI * t : MINI * (t + 1)], grad)
                d = a * ck - b * target
                centred = centred - eta * tn(d.astype(bf16), hb[MINI:])
                qq = qprev if t == 0 else qs[t - 1]
                answer = qq.astype(f32) + c[:MINI] * rho[:MINI]
                if t == 0:
                    zst[before, pl.ds(offs[3], MINI), 0:HS] = answer
                else:
                    zst[s, pl.ds(offs[t - 1], MINI), 0:HS] = answer
            grad = jnp.concatenate(grads, 0)
            first[...] = (layer_one.astype(f32) - eta * tn(keys, grad)).astype(bf16)
            second[...] = (centred + mu).astype(bf16)

            @pl.when(j >= 1)
            def _():
                give_answers(j - 1)
                give_out_weight(j)

            return qs[3]

        qlast = lax.fori_loop(0, SEGS, segment, jnp.zeros((MINI, HS), bf16))
        layer_two = second[...].astype(f32)
        centred = (layer_two - jnp.mean(layer_two, 0, keepdims=True)).astype(bf16)
        h = gelu_parts(nn(qlast, first[...]))[0]
        c = nt(h.astype(bf16), centred)
        rho = lax.rsqrt(jnp.mean(c * c, -1, keepdims=True) + EPS)
        zst[seg_of(SEGS - 1), pl.ds(offs[3], MINI), 0:HS] = qlast.astype(f32) + c * rho
        give_answers(SEGS - 1)

    @pl.when(jnp.logical_not(is_owner))
    def _():
        def one(i, carry):
            give_out_weight(i)
            return carry

        lax.fori_loop(1, SEGS, one, 0)

    for i in range(8):
        landed(zbuf.at[i], z_recv.at[i])
    for v in range(VIDEOS):
        pair = [(zbuf[2 * v + h, :, 0:HS] + zbuf[4 + 2 * v + h, :, 0:HS]).astype(bf16) for h in range(2)]
        heads[vid, ROWS * v : ROWS * (v + 1)] = jnp.concatenate(pair, 1)

    def give_heads(i, carry):
        remote(heads.at[vid], heads.at[vid], h_send.at[i], h_recv.at[vid], video=(vid + i) % GROUPS).start()
        return carry

    lax.fori_loop(1, GROUPS, give_heads, 0)

    def out_weight_landed(i, carry):
        r = (me + i) % SEGS
        landed(owall.at[pl.ds(pl.multiple_of(r * 64, 64), 64)], o_recv.at[r])
        return carry

    lax.fori_loop(1, SEGS, out_weight_landed, 0)

    def project(i, total):
        g = (vid + i) % GROUPS

        @pl.when(i > 0)
        def _():
            landed(heads.at[g], h_recv.at[g])

        return total + nn(heads[g], owall[pl.ds(pl.multiple_of(g * 128, 128), 128)])

    total = lax.fori_loop(0, GROUPS, project, jnp.zeros((VIDEOS * ROWS, 192), f32))
    out_ref[...] = total.astype(bf16)

    for k in range(3):
        remote(w_ref, wall.at[me], y_send.at[k], w_recv.at[me], seg=right).wait_send()

    def sent(chunk, which):
        remote(wall.at[chunk], wall.at[chunk], w_send.at[chunk, which], w_recv.at[chunk], seg=right).wait_send()

    def near_sent(k, carry):
        for which in range(3):
            sent(at(x, y_of(k), core), which)
        for i in (1, 2, 3):
            sent(at(x + i, y_of(k), core), 2)
        row = y_of(k)

        @pl.when(row < 2)
        def _():
            sent(at(x + 3, row, core), 0)

        @pl.when(row >= 2)
        def _():
            sent(at(x + 1, row, core), 1)

        return carry

    lax.fori_loop(0, 4, near_sent, 0)

    def given(i, carry):
        @pl.when(owner_of(i) != me)
        def _():
            remote(qmsg.at[i % 4], qin.at[me], q_send.at[i], q_recv.at[me], seg=right).wait_send()

        return carry

    lax.fori_loop(0, 8, given, 0)

    def out_given(i, carry):
        remote(ow_ref, ow_ref, o_send.at[i], o_recv.at[me], seg=right).wait_send()
        return carry

    lax.fori_loop(1, SEGS, out_given, 0)

    @pl.when(is_owner)
    def _():
        def answered(s, carry):
            @pl.when(s != me)
            def _():
                remote(zst.at[s], zbuf.at[slot], z_send.at[s], z_recv.at[slot], seg=right).wait_send()

            return carry

        lax.fori_loop(0, SEGS, answered, 0)

    def heads_given(i, carry):
        remote(heads.at[vid], heads.at[vid], h_send.at[i], h_recv.at[vid], video=vid).wait_send()
        return carry

    lax.fori_loop(1, GROUPS, heads_given, 0)


def per_device(
    tokens, prompt_ids, prompt_table, qkv_weight, out_weight, init_first, init_second, inner_rate
):
    vmem = pl.BlockSpec(memory_space=pltpu.VMEM)
    smem = pl.BlockSpec(memory_space=pltpu.SMEM)
    dma = pltpu.SemaphoreType.DMA
    mixed = pl.pallas_call(
        kernel,
        out_shape=jax.ShapeDtypeStruct((VIDEOS * ROWS, 192), bf16),
        in_specs=[smem, smem, pl.BlockSpec(memory_space=pl.ANY)] + [vmem] * 5,
        out_specs=vmem,
        scratch_shapes=[
            pltpu.VMEM((VIDEOS, ROWS, 3072), bf16),
            pltpu.VMEM((SEGS, VIDEOS * ROWS, 128), bf16),
            pltpu.VMEM((SEGS, 96, 384), bf16),
            pltpu.VMEM((VIDEOS * ROWS, 384), f32),
            pltpu.VMEM((4, 3, ROWS, 128), bf16),
            pltpu.VMEM((SEGS, 3, ROWS, 128), bf16),
            pltpu.VMEM((SEGS + 1, ROWS, 128), f32),
            pltpu.VMEM((8, ROWS, 128), f32),
            pltpu.VMEM((2048, 192), bf16),
            pltpu.VMEM((GROUPS, VIDEOS * ROWS, 128), bf16),
            pltpu.VMEM((HS, 256), bf16),
            pltpu.VMEM((HS, 256), bf16),
            dma,
            dma((SEGS, 3)),
            dma((SEGS,)),
            dma((3,)),
            dma((8,)),
            dma((SEGS,)),
            dma((SEGS,)),
            dma((SEGS,)),
            dma((SEGS,)),
            dma((8,)),
            dma((GROUPS,)),
            dma((GROUPS,)),
        ],
        compiler_params=pltpu.CompilerParams(
            collective_id=0, has_side_effects=True, vmem_limit_bytes=40 << 20
        ),
        name="chains",
    )(
        inner_rate,
        prompt_ids,
        tokens,
        prompt_table,
        qkv_weight.reshape(96, 384),
        out_weight,
        init_first,
        init_second,
    )
    return mixed.reshape(VIDEOS, ROWS, 192)


def solution(mesh):
    return jax.shard_map(
        per_device,
        mesh=mesh,
        in_specs=(
            P(None, "seg", None),
            P(None, "seg"),
            P(),
            P("seg", None, "video"),
            P("seg", "video"),
            P("video", None, None),
            P("video", None, None),
            P("video"),
        ),
        out_specs=P(None, "seg", "video"),
        check_vma=False,
    )
```

```python
import jax
import jax.numpy as jnp
from jax import lax
from jax.experimental import pallas as pl
from jax.experimental.pallas import tpu as pltpu
from jax.sharding import PartitionSpec as P

HS = 64
MINI = 16
SEGS = 32
GROUPS = 16
VIDEOS = 2
ROWS = 64
EPS = 1e-6
OWN = 4
WORKERS = SEGS - 2 * OWN
C0 = 0.7978845608028654
C1 = C0 * 0.044715
f32 = jnp.float32
bf16 = jnp.bfloat16


def contract(a, b, da, db):
    return lax.dot_general(a, b, (((da,), (db,)), ((), ())), preferred_element_type=f32)


def nn(a, b):
    return contract(a, b, 1, 0)


def nt(a, b):
    return contract(a, b, 1, 1)


def tn(a, b):
    return contract(a, b, 0, 0)


def gelu_parts(x):
    x2 = x * x
    t = jnp.tanh(x * (C0 + C1 * x2))
    half = 0.5 * x
    return half + half * t, t, x2, half


def gelu_slope(t, x2, half):
    return (0.5 + 0.5 * t) + half * (1.0 - t * t) * (C0 + (3.0 * C1) * x2)


def remote(src, dst, send, recv, seg=None, video=None):
    where = {"seg": seg} if video is None else {"video": video}
    return pltpu.make_async_remote_copy(
        src_ref=src,
        dst_ref=dst,
        send_sem=send,
        recv_sem=recv,
        device_id=where,
        device_id_type=pl.DeviceIdType.MESH,
    )


def arrived(ref, sem):
    pltpu.make_async_copy(ref, ref, sem).wait()


def tell(sem, **where):
    pl.semaphore_signal(sem, inc=1, device_id=where, device_id_type=pl.DeviceIdType.MESH)


def kernel(
    rate_ref,
    ids_ref,
    tok_ref,
    table_ref,
    w_ref,
    ow_ref,
    first_ref,
    second_ref,
    out_ref,
    tok,
    table,
    xin,
    wall,
    acc,
    qmsg,
    qin,
    zst,
    zbuf,
    ow,
    owall,
    heads,
    res,
    land,
    first,
    second,
    grads,
    q_pre,
    q_cross,
    tok_sem,
    table_sem,
    w_sem,
    state_sem,
    ow_sem,
    w_send,
    w_recv,
    q_send,
    q_recv,
    o_send,
    o_recv,
    z_send,
    z_recv,
    h_send,
    h_recv,
    a_recv,
    r_send,
    r_recv,
    ring_sem,
):
    me = lax.axis_index("seg")
    vid = lax.axis_index("video")
    core = me % 2
    chip = me // 2
    x = chip // 4
    y = chip % 4
    is_owner = jnp.logical_or(me < OWN, me >= SEGS - OWN)
    is_worker = jnp.logical_not(is_owner)
    head = me % 2

    def at(xx, yy, cc):
        return ((xx % 4) * 4 + yy) * 2 + cc

    loads = [
        pltpu.make_async_copy(w_ref.at[j], wall.at[me, :, pl.ds(128 * j, 128)], w_sem) for j in range(3)
    ]
    loads.append(pltpu.make_async_copy(tok_ref, tok, tok_sem))
    loads.append(pltpu.make_async_copy(table_ref, table, table_sem))
    loads.append(pltpu.make_async_copy(first_ref.at[head], first, state_sem.at[0]))
    loads.append(pltpu.make_async_copy(second_ref.at[head], second, state_sem.at[1]))
    loads.append(pltpu.make_async_copy(ow_ref, ow, ow_sem))
    for load in loads:
        load.start()

    right, left, mate = at(x + 1, y, core), at(x + 3, y, core), at(x, y, 1 - core)
    y1 = y + 1 - 2 * (y % 2)
    y2 = (y + 2) % 4
    y3 = 3 - y
    ring = (vid // 8) * 8
    upper = ring + (vid + 1) % 8
    lower = ring + (vid + 7) % 8
    across = (vid + 8) % 16

    barrier = pltpu.get_barrier_semaphore()
    for target in (at(x, y1, core), at(x, y2, core), at(x, y3, core), right, left, mate):
        tell(barrier, seg=target)

    @pl.when(is_worker)
    def _():
        for target in (upper, lower, across):
            tell(barrier, video=target)

    lane = lax.broadcasted_iota(jnp.int32, (16, 16), 1)
    picks = [jnp.where(lane == ids_ref[0, v], 1.0, 0.0).astype(bf16) for v in range(VIDEOS)]

    def prepare(g, carry):
        span = pl.ds(pl.multiple_of(g * 384, 128), 384)
        for v in range(VIDEOS):
            bias = nn(picks[v], table[:, span])[0:1]
            part = (tok[v, :, span].astype(f32) + bias).astype(bf16)
            for i in range(4):
                xin[g * 4 + i, ROWS * v : ROWS * (v + 1), 0:96] = part[:, 96 * i : 96 * (i + 1)]
        return carry

    loads[3].wait()
    loads[4].wait()
    lax.fori_loop(0, 8, prepare, 0)
    acc[...] = jnp.zeros_like(acc)
    arrived(wall.at[me], w_sem)
    pl.semaphore_wait(barrier, jnp.where(is_worker, 9, 6))

    def y_of(k):
        return jnp.where(k == 0, y, jnp.where(k == 1, y1, jnp.where(k == 2, y2, y3)))

    def pass_on(chunk, target):
        remote(wall.at[chunk], wall.at[chunk], w_send, w_recv.at[chunk], seg=target).start()

    for target in (right, left, at(x, y1, core), at(x, y2, core), at(x, y3, core), mate):
        pass_on(me, target)

    def landed(chunk):
        arrived(wall.at[chunk], w_recv.at[chunk])

    def add(chunk):
        acc[...] += nn(xin[chunk, :, 0:96], wall[chunk])

    def y_step(k, carry):
        chunk = at(x, y_of(k), core)
        landed(chunk)
        pass_on(chunk, right)
        pass_on(chunk, left)
        pass_on(chunk, mate)
        return carry

    def x_step(k, carry):
        @pl.when(k < 3)
        def _():
            y_step(k + 1, 0)

        row = y_of(k)
        a = at(x + 3, row, core)
        b = at(x + 1, row, core)
        landed(a)

        @pl.when(row < 2)
        def _():
            pass_on(a, right)

        pass_on(a, mate)
        landed(b)

        @pl.when(row >= 2)
        def _():
            pass_on(b, left)

        pass_on(b, mate)
        add(at(x, row, core))
        add(a)
        add(b)
        c = at(x, row, 1 - core)
        landed(c)
        add(c)
        return carry

    lax.fori_loop(0, 4, x_step, 0)

    def far_step(k, carry):
        row = y_of(k)
        a = at(x + 2, row, core)
        landed(a)
        pass_on(a, mate)
        add(a)
        for i in (1, 3):
            c = at(x + i, row, 1 - core)
            landed(c)
            add(c)
        return carry

    lax.fori_loop(0, 4, far_step, 0)

    def last_step(k, carry):
        c = at(x + 2, y_of(k), 1 - core)
        landed(c)
        add(c)
        return carry

    lax.fori_loop(0, 4, last_step, 0)

    low = lax.broadcasted_iota(jnp.int32, (1, 128), 1) < HS
    full = [acc[:, 128 * j : 128 * (j + 1)] for j in range(3)]
    turned = [pltpu.roll(part, HS, 1) for part in full]
    for v in range(VIDEOS):
        q, k, val = [part[ROWS * v : ROWS * (v + 1)] for part in full]
        qt, kt, vt = [part[ROWS * v : ROWS * (v + 1)] for part in turned]
        for h in range(2):
            kq = jnp.where(low, k, qt) if h == 0 else jnp.where(low, kt, q)
            kq = kq.astype(bf16)
            for back in range(2):
                n = 4 * back + 2 * v + h
                order = [3, 2, 1, 0] if back else [0, 1, 2, 3]
                for t in range(4):
                    o = order[t]
                    qmsg[n, MINI * t : MINI * (t + 1)] = kq[MINI * o : MINI * (o + 1)]
                for t in range(2):
                    o, p = order[t], order[t + 2]
                    one, two = slice(MINI * o, MINI * (o + 1)), slice(MINI * p, MINI * (p + 1))
                    pair = jnp.where(low, val[one], vt[two]) if h == 0 else jnp.where(low, vt[one], val[two])
                    qmsg[n, ROWS + MINI * t : ROWS + MINI * (t + 1)] = pair.astype(bf16)

    def give(i):
        owner = jnp.where(i < 4, i, SEGS - 8 + i)

        @pl.when(owner == me)
        def _():
            pltpu.make_async_copy(qmsg.at[i], qin.at[me], q_recv.at[me]).start()

        @pl.when(owner != me)
        def _():
            remote(qmsg.at[i], qin.at[me], q_send.at[i], q_recv.at[me], seg=owner).start()

    def given(i):
        @pl.when(jnp.where(i < 4, i, SEGS - 8 + i) != me)
        def _():
            remote(qmsg.at[i], qin.at[me], q_send.at[i], q_recv.at[me], seg=right).wait_send()

    def give_soon(n, carry):
        give(jnp.where(me < 16, n, n + 4))
        return carry

    def give_later(n, carry):
        give(jnp.where(me < 16, n + 4, n))
        return carry

    def soon_given(n, carry):
        given(jnp.where(me < 16, n, n + 4))
        return carry

    def later_given(n, carry):
        given(jnp.where(me < 16, n + 4, n))
        return carry

    lax.fori_loop(0, 4, give_soon, 0)

    @pl.when(is_worker)
    def _():
        lax.fori_loop(0, 4, soon_given, 0)

    lax.fori_loop(0, 4, give_later, 0)

    loads[-1].wait()
    my_rows = pl.ds(pl.multiple_of(me * 64, 64), 64)

    def give_out_weight(i):
        target = OWN + (i + me) % WORKERS
        remote(ow, owall.at[my_rows], o_send, o_recv, seg=target).start()

    def piece_place(s, t):
        upper_half = jnp.where(s < 16, 0, 1)
        i = jnp.where(s < 16, 4 * s + t, 4 * (SEGS - 1 - s) + 3 - t)
        p = i % 12
        return OWN + 12 * upper_half + (p % 6) * 2 + p // 6, i // 12

    @pl.when(is_owner)
    def _():
        back = jnp.where(me < OWN, 0, 1)
        slot = jnp.where(me < OWN, me, me - (SEGS - 8))
        eta = rate_ref[head]
        loads[5].wait()
        loads[6].wait()

        def seg_of(j):
            return j + back * (SEGS - 1 - 2 * j)

        def give_answer(j, t):
            s = seg_of(j)
            target, place = piece_place(s, t + back * (3 - 2 * t))
            remote(zst.at[j, t], zbuf.at[place, slot], z_send, z_recv.at[place], seg=target).start()

        grads[...] = jnp.zeros_like(grads)
        q_pre[...] = jnp.zeros_like(q_pre)
        q_cross[...] = jnp.zeros_like(q_cross)

        def wait_for(j):
            s = seg_of(j)
            arrived(qin.at[s], q_recv.at[s])

        def segment(j, pre, begin=False, end=False):
            if not end:
                wait_for(j + 1)
            before = j if begin else j - 1
            s, s_before, s_next = seg_of(j), seg_of(before), seg_of(j if end else j + 1)
            keys = qin[s, 0:ROWS, 0:HS]
            queries = qin[s, 0:ROWS, HS:128]
            values = jnp.concatenate([qin[s, ROWS:96, 0:HS], qin[s, ROWS:96, HS:128]], 0)
            keys_before = qin[s_before, 0:ROWS, 0:HS]
            last_query = qin[s_before, 48:ROWS, HS:128]
            keys_ahead = jnp.concatenate([keys[MINI:], qin[s_next, 0:MINI, 0:HS]], 0)
            grads_before = grads[...]
            layer_one = (first[...].astype(f32) - eta * tn(keys_before, grads_before)).astype(bf16)
            first[...] = layer_one
            pre_q = q_pre[...] + nn(q_cross[...], grads_before)
            base_k = nn(keys_ahead, layer_one)
            base_q = nn(queries, layer_one)
            cross = -eta * nt(keys_ahead, keys)
            cross_b = cross.astype(bf16)
            cross_q = (-eta * nt(queries, keys)).astype(bf16)
            targets = values.astype(f32) - keys.astype(f32)
            targets = targets - jnp.mean(targets, -1, keepdims=True)
            layer_two = second[...].astype(f32)
            mu = jnp.mean(layer_two, 0, keepdims=True)
            centred = layer_two - mu
            ahead = [base_k[MINI * t : MINI * (t + 1)] for t in range(4)]
            done = []
            for t in range(4):
                rows = slice(MINI * t, MINI * (t + 1))
                h, th, x2, half = gelu_parts(pre)
                hb = h.astype(bf16)
                weights = centred.astype(bf16)
                target = targets[rows]
                c = nt(hb, weights)
                w = nn(target.astype(bf16), weights)
                u = nn(c.astype(bf16), weights)
                rho = lax.rsqrt(jnp.mean(c * c, -1, keepdims=True) + EPS)
                m = jnp.mean(target * c, -1, keepdims=True)
                r2 = rho * rho
                b = rho * (1.0 / MINI)
                a = (r2 * (1.0 / MINI)) * (EPS * r2 + rho * m)
                ct = nt(weights, hb)
                target_t = target.T
                rho_t = lax.rsqrt(jnp.sum(ct * ct, 0, keepdims=True) * (1.0 / HS) + EPS)
                m_t = jnp.sum(target_t * ct, 0, keepdims=True) * (1.0 / HS)
                r2_t = rho_t * rho_t
                b_t = rho_t * (eta / MINI)
                a_t = (r2_t * (-eta / MINI)) * (EPS * r2_t + rho_t * m_t)
                moved = centred + nn((a_t * ct + b_t * target_t).astype(bf16), hb)
                slope = gelu_slope(th, x2, half)
                grad = a * (u * slope) - b * (w * slope)
                grad_b = grad.astype(bf16)
                done.append(grad_b)
                sums = [ahead[t], None]
                for i in range(MINI):
                    col = cross[rows, MINI * t + i : MINI * t + i + 1]
                    term = jnp.broadcast_to(col, (MINI, 256)) * jnp.broadcast_to(grad[i : i + 1], (MINI, 256))
                    sums[i % 2] = term if sums[i % 2] is None else sums[i % 2] + term
                pre = sums[0] + sums[1]
                for r in range(t + 1, 4):
                    ahead[r] = ahead[r] + nn(cross_b[MINI * r : MINI * (r + 1), rows], grad_b)
                hq = gelu_parts(pre_q)[0]
                cq = nt(hq.astype(bf16), weights)
                rho_q = lax.rsqrt(jnp.mean(cq * cq, -1, keepdims=True) + EPS)
                if t == 0:
                    zst[before, 3, :, 0:HS] = last_query.astype(f32) + cq * rho_q
                else:
                    zst[j, t - 1, :, 0:HS] = queries[MINI * (t - 1) : MINI * t].astype(f32) + cq * rho_q
                if t < 3:
                    so_far = jnp.concatenate(done, 0) if t else grad_b
                    pre_q = base_q[rows] + nn(cross_q[rows, : MINI * (t + 1)], so_far)
                centred = moved
            grads[...] = jnp.concatenate(done, 0)
            q_pre[...] = base_q[48:ROWS]
            q_cross[...] = cross_q[48:ROWS]
            second[...] = (centred + mu).astype(bf16)
            if not begin:
                give_answer(before, 3)
            for t in range(3):
                give_answer(j, t)
            return pre

        def send_out_weight(i, carry):
            give_out_weight(i)
            return carry

        lax.fori_loop(0, WORKERS, send_out_weight, 0)
        wait_for(0)
        pre = nn(qin[seg_of(0), 0:MINI, 0:HS], first[...])
        pre = segment(0, pre, begin=True)
        pre = lax.fori_loop(1, SEGS - 1, segment, pre)
        segment(SEGS - 1, pre, end=True)
        pre_q = q_pre[...] + nn(q_cross[...], grads[...])
        layer_two = second[...].astype(f32)
        centred = (layer_two - jnp.mean(layer_two, 0, keepdims=True)).astype(bf16)
        c = nt(gelu_parts(pre_q)[0].astype(bf16), centred)
        rho = lax.rsqrt(jnp.mean(c * c, -1, keepdims=True) + EPS)
        zst[SEGS - 1, 3, :, 0:HS] = qin[seg_of(SEGS - 1), 48:ROWS, HS:128].astype(f32) + c * rho
        give_answer(SEGS - 1, 3)

    @pl.when(is_worker)
    def _():
        lax.fori_loop(0, 4, later_given, 0)

        def send_out_weight(i, carry):
            @pl.when(OWN + (i + me) % WORKERS != me)
            def _():
                give_out_weight(i)

            return carry

        lax.fori_loop(0, WORKERS, send_out_weight, 0)
        pltpu.make_async_copy(ow, owall.at[my_rows], o_recv).start()

        for k in range(3):
            tell(ring_sem.at[k], video=upper)
            tell(ring_sem.at[k], video=lower)
            pl.semaphore_wait(ring_sem.at[k], 2)
        tell(ring_sem.at[3], video=across)
        pl.semaphore_wait(ring_sem.at[3], 1)

        arrived(owall, o_recv)
        upper_half = jnp.where(me < 16, 0, 1)
        r = me - OWN - 12 * upper_half
        p = r // 2 + 6 * (r % 2)
        count = jnp.where(p < 4, 6, 5)
        mine = pl.ds(pl.multiple_of(vid * 128, 128), 128)
        theirs = pl.ds(pl.multiple_of(across * 128, 128), 128)

        def place_of(n):
            place = count - 1 - n
            i = 12 * place + p
            s = jnp.where(upper_half == 0, i // 4, SEGS - 1 - i // 4)
            t = jnp.where(upper_half == 0, i % 4, 3 - i % 4)
            return place, s, t

        def spread(place, columns):
            block = heads.at[place, :, columns]

            def one(d, carry):
                remote(
                    block, block, h_send.at[place], h_recv.at[place], video=ring + (vid + d) % 8
                ).start()
                return carry

            lax.fori_loop(1, 8, one, 0)

        def gather(n):
            place, _, _ = place_of(n)
            arrived(zbuf.at[place], z_recv.at[place])
            for v in range(VIDEOS):
                pair = [zbuf[place, 2 * v + h, :, 0:HS] + zbuf[place, 4 + 2 * v + h, :, 0:HS] for h in range(2)]
                heads[place, MINI * v : MINI * (v + 1), mine] = jnp.concatenate(pair, 1).astype(bf16)
            block = heads.at[place, :, mine]
            remote(block, block, h_send.at[place], a_recv.at[place], video=across).start()
            spread(place, mine)

        def relay(n):
            place, _, _ = place_of(n)
            arrived(heads.at[place, :, theirs], a_recv.at[place])
            spread(place, theirs)

        def finish(n):
            place, s, t = place_of(n)
            arrived(heads.at[place, :, pl.ds(0, 128 * 14)], h_recv.at[place])
            res[place] = nn(heads[place], owall[...]).astype(bf16)

            @pl.when(s == me)
            def _():
                pltpu.make_async_copy(res.at[place], land.at[t], r_recv).start()

            @pl.when(s != me)
            def _():
                remote(res.at[place], land.at[t], r_send.at[place], r_recv, seg=s).start()

        def piece(n, carry):
            relay(n - 1)
            gather(n)
            finish(n - 1)
            return carry

        gather(0)
        lax.fori_loop(1, count, piece, 0)
        relay(count - 1)
        finish(count - 1)

        def piece_sent(n, carry):
            i = 12 * n + p
            s = jnp.where(upper_half == 0, i // 4, SEGS - 1 - i // 4)
            arrived(heads.at[n, :, pl.ds(0, 128 * (GROUPS - 1))], h_send.at[n])

            @pl.when(s != me)
            def _():
                remote(res.at[n], land.at[0], r_send.at[n], r_recv, seg=s).wait_send()

            return carry

        lax.fori_loop(0, count, piece_sent, 0)
        arrived(owall.at[pl.ds(0, 64 * (WORKERS - 1))], o_send)
        loads[5].wait()
        loads[6].wait()

    @pl.when(is_owner)
    def _():
        lax.fori_loop(0, 4, soon_given, 0)
        lax.fori_loop(0, 4, later_given, 0)
        arrived(owall.at[pl.ds(0, 64 * WORKERS)], o_send)
        arrived(zst, z_send)

    arrived(wall.at[pl.ds(0, SEGS - 1)], w_send)

    arrived(land, r_recv)
    for t in range(4):
        for v in range(VIDEOS):
            out_ref[v, MINI * t : MINI * (t + 1)] = land[t, MINI * v : MINI * (v + 1)]


def per_device(
    tokens, prompt_ids, prompt_table, qkv_weight, out_weight, init_first, init_second, inner_rate
):
    vmem = pl.BlockSpec(memory_space=pltpu.VMEM)
    smem = pl.BlockSpec(memory_space=pltpu.SMEM)
    hbm = pl.BlockSpec(memory_space=pltpu.HBM)
    dma = pltpu.SemaphoreType.DMA
    return pl.pallas_call(
        kernel,
        out_shape=jax.ShapeDtypeStruct((VIDEOS, ROWS, 192), bf16),
        in_specs=[smem, smem] + [hbm] * 6,
        out_specs=vmem,
        scratch_shapes=[
            pltpu.VMEM((VIDEOS, ROWS, 3072), bf16),
            pltpu.VMEM((16, 3072), bf16),
            pltpu.VMEM((SEGS, VIDEOS * ROWS, 128), bf16),
            pltpu.VMEM((SEGS, 96, 384), bf16),
            pltpu.VMEM((VIDEOS * ROWS, 384), f32),
            pltpu.VMEM((8, 96, 128), bf16),
            pltpu.VMEM((SEGS, 96, 128), bf16),
            pltpu.VMEM((SEGS, 4, MINI, 128), f32),
            pltpu.VMEM((6, 8, MINI, 128), f32),
            pltpu.VMEM((64, 192), bf16),
            pltpu.VMEM((2048, 192), bf16),
            pltpu.VMEM((6, VIDEOS * MINI, 2048), bf16),
            pltpu.VMEM((6, VIDEOS * MINI, 192), bf16),
            pltpu.VMEM((4, VIDEOS * MINI, 192), bf16),
            pltpu.VMEM((HS, 256), bf16),
            pltpu.VMEM((HS, 256), bf16),
            pltpu.VMEM((ROWS, 256), bf16),
            pltpu.VMEM((MINI, 256), f32),
            pltpu.VMEM((MINI, HS), bf16),
            dma,
            dma,
            dma,
            dma((2,)),
            dma,
            dma,
            dma((SEGS,)),
            dma((8,)),
            dma((SEGS,)),
            dma,
            dma,
            dma,
            dma((6,)),
            dma((6,)),
            dma((6,)),
            dma((6,)),
            dma((6,)),
            dma,
            pltpu.SemaphoreType.REGULAR((4,)),
        ],
        compiler_params=pltpu.CompilerParams(
            collective_id=0, has_side_effects=True, vmem_limit_bytes=60 << 20
        ),
        name="chains",
    )(
        inner_rate,
        prompt_ids.T,
        tokens,
        prompt_table,
        jnp.transpose(qkv_weight, (1, 0, 2)),
        out_weight,
        init_first,
        init_second,
    )


def solution(mesh):
    return jax.shard_map(
        per_device,
        mesh=mesh,
        in_specs=(
            P(None, "seg", None),
            P(None, "seg"),
            P(),
            P("seg", None, "video"),
            P("seg", "video"),
            P("video", None, None),
            P("video", None, None),
            P("video"),
        ),
        out_specs=P(None, "seg", "video"),
        check_vma=False,
    )
```

```python
import jax
import jax.numpy as jnp
from jax import lax
from jax.experimental import pallas as pl
from jax.experimental.pallas import tpu as pltpu
from jax.sharding import PartitionSpec as P

HS = 64
MINI = 16
SEGS = 32
GROUPS = 16
VIDEOS = 2
ROWS = 64
EPS = 1e-6
OWN = 4
WORKERS = SEGS - 2 * OWN
PARTS = 1
PART = 96 // PARTS
C0 = 0.7978845608028654
C1 = C0 * 0.044715
f32 = jnp.float32
bf16 = jnp.bfloat16


def contract(a, b, da, db):
    return lax.dot_general(a, b, (((da,), (db,)), ((), ())), preferred_element_type=f32)


def nn(a, b):
    return contract(a, b, 1, 0)


def nt(a, b):
    return contract(a, b, 1, 1)


def tn(a, b):
    return contract(a, b, 0, 0)


def gelu_parts(x):
    x2 = x * x
    t = jnp.tanh(x * (C0 + C1 * x2))
    half = 0.5 * x
    return half + half * t, t, x2, half


def gelu_slope(t, x2, half):
    return (0.5 + 0.5 * t) + half * (1.0 - t * t) * (C0 + (3.0 * C1) * x2)


def remote(src, dst, send, recv, seg=None, video=None):
    where = {"seg": seg} if video is None else {"video": video}
    return pltpu.make_async_remote_copy(
        src_ref=src,
        dst_ref=dst,
        send_sem=send,
        recv_sem=recv,
        device_id=where,
        device_id_type=pl.DeviceIdType.MESH,
    )


def arrived(ref, sem):
    pltpu.make_async_copy(ref, ref, sem).wait()


def tell(sem, **where):
    pl.semaphore_signal(sem, inc=1, device_id=where, device_id_type=pl.DeviceIdType.MESH)


def kernel(
    rate_ref,
    ids_ref,
    tok_ref,
    table_ref,
    w_ref,
    ow_ref,
    first_ref,
    second_ref,
    out_ref,
    tok,
    table,
    xin,
    wall,
    acc,
    qmsg,
    qin,
    zst,
    zbuf,
    ow,
    owall,
    heads,
    res,
    land,
    first,
    second,
    grads,
    q_weights,
    p_query,
    p_target,
    p_across,
    p_turned,
    tok_sem,
    table_sem,
    w_sem,
    state_sem,
    ow_sem,
    w_send,
    w_recv,
    q_send,
    q_recv,
    o_send,
    o_recv,
    z_send,
    z_recv,
    h_send,
    h_recv,
    a_recv,
    r_send,
    r_recv,
    ring_sem,
):
    me = lax.axis_index("seg")
    vid = lax.axis_index("video")
    core = me % 2
    chip = me // 2
    x = chip // 4
    y = chip % 4
    is_owner = jnp.logical_or(me < OWN, me >= SEGS - OWN)
    is_worker = jnp.logical_not(is_owner)
    head = me % 2

    def at(xx, yy, cc):
        return ((xx % 4) * 4 + yy) * 2 + cc

    loads = [
        pltpu.make_async_copy(w_ref.at[j], wall.at[me, :, pl.ds(128 * j, 128)], w_sem) for j in range(3)
    ]
    loads.append(pltpu.make_async_copy(tok_ref, tok, tok_sem))
    loads.append(pltpu.make_async_copy(table_ref, table, table_sem))
    loads.append(pltpu.make_async_copy(first_ref.at[head], first, state_sem.at[0]))
    loads.append(pltpu.make_async_copy(second_ref.at[head], second, state_sem.at[1]))
    loads.append(pltpu.make_async_copy(ow_ref, ow, ow_sem))
    for load in loads:
        load.start()

    right, left, mate = at(x + 1, y, core), at(x + 3, y, core), at(x, y, 1 - core)
    y1 = y + 1 - 2 * (y % 2)
    y2 = (y + 2) % 4
    y3 = 3 - y
    ring = (vid // 8) * 8
    upper = ring + (vid + 1) % 8
    lower = ring + (vid + 7) % 8
    across = (vid + 8) % 16

    barrier = pltpu.get_barrier_semaphore()
    for target in (at(x, y1, core), at(x, y2, core), at(x, y3, core), right, left, mate):
        tell(barrier, seg=target)

    @pl.when(is_worker)
    def _():
        for target in (upper, lower, across):
            tell(barrier, video=target)

    lane = lax.broadcasted_iota(jnp.int32, (16, 16), 1)
    picks = [jnp.where(lane == ids_ref[0, v], 1.0, 0.0).astype(bf16) for v in range(VIDEOS)]

    def prepare(g, carry):
        span = pl.ds(pl.multiple_of(g * 384, 128), 384)
        for v in range(VIDEOS):
            bias = nn(picks[v], table[:, span])[0:1]
            part = (tok[v, :, span].astype(f32) + bias).astype(bf16)
            for i in range(4):
                xin[g * 4 + i, ROWS * v : ROWS * (v + 1), 0:96] = part[:, 96 * i : 96 * (i + 1)]
        return carry

    loads[3].wait()
    loads[4].wait()
    lax.fori_loop(0, 8, prepare, 0)
    acc[...] = jnp.zeros_like(acc)
    arrived(wall.at[me], w_sem)
    pl.semaphore_wait(barrier, jnp.where(is_worker, 9, 6))

    def y_of(k):
        return jnp.where(k == 0, y, jnp.where(k == 1, y1, jnp.where(k == 2, y2, y3)))

    def half_of(chunk, part):
        return wall.at[chunk, pl.ds(PART * part, PART)]

    def pass_on(chunk, part, target):
        block = half_of(chunk, part)
        remote(block, block, w_send, w_recv.at[chunk, part], seg=target).start()

    def start_lines(part):
        for target in (at(x, y1, core), at(x, y2, core), at(x, y3, core)):
            pass_on(me, part, target)

    start_lines(0)
    for part in range(PARTS):
        pass_on(me, part, right)
        pass_on(me, part, left)

    def landed(chunk, part):
        arrived(half_of(chunk, part), w_recv.at[chunk, part])

    def add(chunk):
        acc[...] += nn(xin[chunk, :, 0:96], wall[chunk])

    def y_step(part):
        def one(k, carry):
            chunk = at(x, y_of(k), core)
            landed(chunk, part)
            pass_on(chunk, part, right)
            pass_on(chunk, part, left)
            pass_on(chunk, part, mate)
            return carry

        one(1, 0)
        if part + 1 < PARTS:
            start_lines(part + 1)
        pass_on(me, part, mate)
        lax.fori_loop(2, 4, one, 0)

    def x_step(k, part):
        row = y_of(k)
        a = at(x + 3, row, core)
        b = at(x + 1, row, core)
        landed(a, part)
        to_right = (row + part) % 2 == 0

        @pl.when(to_right)
        def _():
            pass_on(a, part, right)

        pass_on(a, part, mate)
        landed(b, part)

        @pl.when(jnp.logical_not(to_right))
        def _():
            pass_on(b, part, left)

        pass_on(b, part, mate)

    def add_near(k, carry):
        add(at(x, y_of(k), core))
        add(at(x + 3, y_of(k), core))
        add(at(x + 1, y_of(k), core))
        return carry

    for part in range(PARTS):
        y_step(part)
        x_step(0, part)

        if part > 0:
            lax.fori_loop(1, 4, lambda k, c: (x_step(k, part - 1), c)[1], 0)
    lax.fori_loop(1, 4, lambda k, c: (x_step(k, PARTS - 1), c)[1], 0)
    lax.fori_loop(0, 4, add_near, 0)

    def other_add(chunk):
        for part in range(PARTS):
            landed(chunk, part)
        add(chunk)

    def far_step(k, carry):
        far = at(x + 2, y_of(k), core)
        for part in range(PARTS):
            landed(far, part)
            pass_on(far, part, mate)
        add(far)
        for i in (0, 1, 3):
            other_add(at(x + i, y_of(k), 1 - core))
        return carry

    lax.fori_loop(0, 4, far_step, 0)

    def last_step(k, carry):
        other_add(at(x + 2, y_of(k), 1 - core))
        return carry

    lax.fori_loop(0, 4, last_step, 0)

    low = lax.broadcasted_iota(jnp.int32, (1, 128), 1) < HS
    full = [acc[:, 128 * j : 128 * (j + 1)].astype(bf16).astype(f32) for j in range(3)]
    wanted = full[2] - full[1]
    mean_low = jnp.sum(jnp.where(low, wanted, 0.0), -1, keepdims=True) * (1.0 / HS)
    mean_high = jnp.sum(jnp.where(low, 0.0, wanted), -1, keepdims=True) * (1.0 / HS)
    full[2] = wanted - jnp.where(low, mean_low, mean_high)
    turned = [pltpu.roll(part, HS, 1) for part in full]
    for v in range(VIDEOS):
        q, k, val = [part[ROWS * v : ROWS * (v + 1)] for part in full]
        qt, kt, vt = [part[ROWS * v : ROWS * (v + 1)] for part in turned]
        for h in range(2):
            kq = jnp.where(low, k, qt) if h == 0 else jnp.where(low, kt, q)
            kq = kq.astype(bf16)
            for back in range(2):
                n = 4 * back + 2 * v + h
                order = [3, 2, 1, 0] if back else [0, 1, 2, 3]
                for t in range(4):
                    o = order[t]
                    qmsg[n, MINI * t : MINI * (t + 1)] = kq[MINI * o : MINI * (o + 1)]
                for t in range(2):
                    o, p = order[t], order[t + 2]
                    one, two = slice(MINI * o, MINI * (o + 1)), slice(MINI * p, MINI * (p + 1))
                    pair = jnp.where(low, val[one], vt[two]) if h == 0 else jnp.where(low, vt[one], val[two])
                    qmsg[n, ROWS + MINI * t : ROWS + MINI * (t + 1)] = pair.astype(bf16)

    def give(i):
        owner = jnp.where(i < 4, i, SEGS - 8 + i)

        @pl.when(owner == me)
        def _():
            pltpu.make_async_copy(qmsg.at[i], qin.at[me], q_recv.at[me]).start()

        @pl.when(owner != me)
        def _():
            remote(qmsg.at[i], qin.at[me], q_send.at[i], q_recv.at[me], seg=owner).start()

    def given(i):
        @pl.when(jnp.where(i < 4, i, SEGS - 8 + i) != me)
        def _():
            remote(qmsg.at[i], qin.at[me], q_send.at[i], q_recv.at[me], seg=right).wait_send()

    def give_soon(n, carry):
        give(jnp.where(me < 16, n, n + 4))
        return carry

    def give_later(n, carry):
        give(jnp.where(me < 16, n + 4, n))
        return carry

    def soon_given(n, carry):
        given(jnp.where(me < 16, n, n + 4))
        return carry

    def later_given(n, carry):
        given(jnp.where(me < 16, n + 4, n))
        return carry

    lax.fori_loop(0, 4, give_soon, 0)

    @pl.when(is_worker)
    def _():
        lax.fori_loop(0, 4, soon_given, 0)

    lax.fori_loop(0, 4, give_later, 0)

    loads[-1].wait()
    my_rows = pl.ds(pl.multiple_of(me * 64, 64), 64)

    def give_out_weight(i):
        target = OWN + (i + me) % WORKERS
        remote(ow, owall.at[my_rows], o_send, o_recv, seg=target).start()

    def piece_place(s, t):
        upper_half = jnp.where(s < 16, 0, 1)
        i = jnp.where(s < 16, 4 * s + t, 4 * (SEGS - 1 - s) + 3 - t)
        p = i % 12
        return OWN + 12 * upper_half + (p % 6) * 2 + p // 6, i // 12

    @pl.when(is_owner)
    def _():
        back = jnp.where(me < OWN, 0, 1)
        slot = jnp.where(me < OWN, me, me - (SEGS - 8))
        eta = rate_ref[head]
        loads[5].wait()
        loads[6].wait()

        def seg_of(j):
            return j + back * (SEGS - 1 - 2 * j)

        def give_answer(j, t):
            s = seg_of(j)
            target, place = piece_place(s, t + back * (3 - 2 * t))
            remote(zst.at[j, t], zbuf.at[place, slot], z_send, z_recv.at[place], seg=target).start()

        grads[...] = jnp.zeros_like(grads)
        row_block = lax.broadcasted_iota(jnp.int32, (ROWS, ROWS), 0) // MINI
        upto = row_block >= lax.broadcasted_iota(jnp.int32, (ROWS, ROWS), 1) // MINI

        def wait_for(j):
            s = seg_of(j)
            arrived(qin.at[s], q_recv.at[s])

        def lay_out(j, slot):
            s = seg_of(j)
            keys = qin[s, 0:ROWS, 0:HS]
            targets = jnp.concatenate([qin[s, ROWS:96, 0:HS], qin[s, ROWS:96, HS:128]], 0)
            p_query[slot] = qin[s, 0:ROWS, HS:128]
            p_turned[slot] = keys.T
            targets = targets.astype(f32)
            p_target[slot] = targets
            for t in range(4):
                p_across[slot, t] = targets[MINI * t : MINI * (t + 1)].T

        def query_hidden(slot, keys, layer_one, grad):
            queries = p_query[slot]
            cross = jnp.where(upto, -eta * nt(queries, keys), 0.0).astype(bf16)
            return gelu_parts(nn(queries, layer_one) + nn(cross, grad))[0].astype(bf16)

        def query_answers(slot, h, j, which):
            for t in which:
                rows = slice(MINI * t, MINI * (t + 1))
                c = nt(h[rows], q_weights[slot, t])
                rho = lax.rsqrt(jnp.mean(c * c, -1, keepdims=True) + EPS)
                zst[j, t, :, 0:HS] = p_query[slot, rows].astype(f32) + c * rho

        def answer_queries(slot, keys, layer_one, grad, j):
            query_answers(slot, query_hidden(slot, keys, layer_one, grad), j, range(4))

        def segment(j, pre, slot, begin=False, end=False):
            if not end:
                wait_for(j + 1)
            s, s_next = seg_of(j), seg_of(j if end else j + 1)
            keys = qin[s, 0:ROWS, 0:HS]
            targets = p_target[slot]
            targets_t = [p_across[slot, t] for t in range(4)]
            keys_ahead = jnp.concatenate([keys[MINI:], qin[s_next, 0:MINI, 0:HS]], 0)
            grads_before = grads[...]
            layer_one = first[...]
            if not begin:
                before = j - 1
                keys_before = qin[seg_of(before), 0:ROWS, 0:HS]
                layer_before = layer_one
                layer_one = (layer_one.astype(f32) - eta * nn(p_turned[1 - slot], grads_before)).astype(bf16)
                first[...] = layer_one
            base_k = nn(keys_ahead, layer_one)
            cross = -eta * nt(keys_ahead, keys)
            cross_b = cross.astype(bf16)
            layer_two = second[...].astype(f32)
            mu = jnp.mean(layer_two, 0, keepdims=True)
            centred = layer_two - mu
            ahead = [base_k[MINI * t : MINI * (t + 1)] for t in range(4)]
            done = []
            for t in range(4):
                rows = slice(MINI * t, MINI * (t + 1))
                h, th, x2, half = gelu_parts(pre)
                hb = h.astype(bf16)
                weights = centred.astype(bf16)
                target = targets[rows]
                c = nt(hb, weights)
                w = nn(target.astype(bf16), weights)
                u = nn(c.astype(bf16), weights)
                rho = lax.rsqrt(jnp.mean(c * c, -1, keepdims=True) + EPS)
                m = jnp.mean(target * c, -1, keepdims=True)
                r2 = rho * rho
                b = rho * (1.0 / MINI)
                a = (r2 * (1.0 / MINI)) * (EPS * r2 + rho * m)
                ct = nt(weights, hb)
                target_t = targets_t[t]
                rho_t = lax.rsqrt(jnp.sum(ct * ct, 0, keepdims=True) * (1.0 / HS) + EPS)
                m_t = jnp.sum(target_t * ct, 0, keepdims=True) * (1.0 / HS)
                r2_t = rho_t * rho_t
                b_t = rho_t * (eta / MINI)
                a_t = (r2_t * (-eta / MINI)) * (EPS * r2_t + rho_t * m_t)
                moved = centred + nn((a_t * ct + b_t * target_t).astype(bf16), hb)
                slope = gelu_slope(th, x2, half)
                grad = a * (u * slope) - b * (w * slope)
                grad_b = grad.astype(bf16)
                done.append(grad_b)
                sums = [ahead[t], None]
                for i in range(MINI):
                    col = cross[rows, MINI * t + i : MINI * t + i + 1]
                    term = jnp.broadcast_to(col, (MINI, 256)) * jnp.broadcast_to(grad[i : i + 1], (MINI, 256))
                    sums[i % 2] = term if sums[i % 2] is None else sums[i % 2] + term
                pre = sums[0] + sums[1]
                for r in range(t + 1, 4):
                    ahead[r] = ahead[r] + nn(cross_b[MINI * r : MINI * (r + 1), rows], grad_b)
                q_weights[slot, t] = moved.astype(bf16)
                centred = moved
                if t == 0 and not begin:
                    h_query = query_hidden(1 - slot, keys_before, layer_before, grads_before)
                if t == 0 and not begin:
                    query_answers(1 - slot, h_query, before, [0])
                if t == 1 and not begin:
                    query_answers(1 - slot, h_query, before, [1])
                if t == 2 and not begin:
                    query_answers(1 - slot, h_query, before, [2])
                if t == 3 and not begin:
                    query_answers(1 - slot, h_query, before, [3])
            grads[...] = jnp.concatenate(done, 0)
            second[...] = (centred + mu).astype(bf16)
            if not end:
                lay_out(j + 1, 1 - slot)
            if not begin:
                for t in range(4):
                    give_answer(before, t)
            return pre

        def send_out_weight(i, carry):
            give_out_weight(i)
            return carry

        lax.fori_loop(0, WORKERS, send_out_weight, 0)
        wait_for(0)
        pre = nn(qin[seg_of(0), 0:MINI, 0:HS], first[...])
        lay_out(0, 0)
        pre = segment(0, pre, 0, begin=True)

        def two_segments(i, pre):
            pre = segment(2 * i + 1, pre, 1)
            return segment(2 * i + 2, pre, 0)

        pre = lax.fori_loop(0, SEGS // 2 - 1, two_segments, pre)
        segment(SEGS - 1, pre, 1, end=True)
        s_last = seg_of(SEGS - 1)
        answer_queries(1, qin[s_last, 0:ROWS, 0:HS], first[...], grads[...], SEGS - 1)
        for t in range(4):
            give_answer(SEGS - 1, t)

    @pl.when(is_worker)
    def _():
        lax.fori_loop(0, 4, later_given, 0)

        def send_out_weight(i, carry):
            @pl.when(OWN + (i + me) % WORKERS != me)
            def _():
                give_out_weight(i)

            return carry

        lax.fori_loop(0, WORKERS, send_out_weight, 0)
        pltpu.make_async_copy(ow, owall.at[my_rows], o_recv).start()

        for k in range(3):
            tell(ring_sem.at[k], video=upper)
            tell(ring_sem.at[k], video=lower)
            pl.semaphore_wait(ring_sem.at[k], 2)
        tell(ring_sem.at[3], video=across)
        pl.semaphore_wait(ring_sem.at[3], 1)

        arrived(owall, o_recv)
        upper_half = jnp.where(me < 16, 0, 1)
        r = me - OWN - 12 * upper_half
        p = r // 2 + 6 * (r % 2)
        count = jnp.where(p < 4, 6, 5)
        mine = pl.ds(pl.multiple_of(vid * 128, 128), 128)
        theirs = pl.ds(pl.multiple_of(across * 128, 128), 128)

        def place_of(n):
            place = count - 1 - n
            i = 12 * place + p
            s = jnp.where(upper_half == 0, i // 4, SEGS - 1 - i // 4)
            t = jnp.where(upper_half == 0, i % 4, 3 - i % 4)
            return place, s, t

        def spread(place, columns):
            block = heads.at[place, :, columns]

            def one(d, carry):
                remote(
                    block, block, h_send.at[place], h_recv.at[place], video=ring + (vid + d) % 8
                ).start()
                return carry

            lax.fori_loop(1, 8, one, 0)

        def gather(n):
            place, _, _ = place_of(n)
            arrived(zbuf.at[place], z_recv.at[place])
            for v in range(VIDEOS):
                pair = [zbuf[place, 2 * v + h, :, 0:HS] + zbuf[place, 4 + 2 * v + h, :, 0:HS] for h in range(2)]
                heads[place, MINI * v : MINI * (v + 1), mine] = jnp.concatenate(pair, 1).astype(bf16)
            block = heads.at[place, :, mine]
            remote(block, block, h_send.at[place], a_recv.at[place], video=across).start()
            spread(place, mine)

        def relay(n):
            place, _, _ = place_of(n)
            arrived(heads.at[place, :, theirs], a_recv.at[place])
            spread(place, theirs)

        def finish(n):
            place, s, t = place_of(n)
            arrived(heads.at[place, :, pl.ds(0, 128 * 14)], h_recv.at[place])
            res[place] = nn(heads[place], owall[...]).astype(bf16)

            @pl.when(s == me)
            def _():
                pltpu.make_async_copy(res.at[place], land.at[t], r_recv).start()

            @pl.when(s != me)
            def _():
                remote(res.at[place], land.at[t], r_send.at[place], r_recv, seg=s).start()

        def piece(n, carry):
            relay(n - 1)
            gather(n)
            finish(n - 1)
            return carry

        gather(0)
        lax.fori_loop(1, count, piece, 0)
        relay(count - 1)
        finish(count - 1)

        def piece_sent(n, carry):
            i = 12 * n + p
            s = jnp.where(upper_half == 0, i // 4, SEGS - 1 - i // 4)
            arrived(heads.at[n, :, pl.ds(0, 128 * (GROUPS - 1))], h_send.at[n])

            @pl.when(s != me)
            def _():
                remote(res.at[n], land.at[0], r_send.at[n], r_recv, seg=s).wait_send()

            return carry

        lax.fori_loop(0, count, piece_sent, 0)
        arrived(owall.at[pl.ds(0, 64 * (WORKERS - 1))], o_send)
        loads[5].wait()
        loads[6].wait()

    @pl.when(is_owner)
    def _():
        lax.fori_loop(0, 4, soon_given, 0)
        lax.fori_loop(0, 4, later_given, 0)
        arrived(owall.at[pl.ds(0, 64 * WORKERS)], o_send)
        arrived(zst, z_send)

    arrived(wall.at[pl.ds(0, SEGS - 1)], w_send)

    arrived(land, r_recv)
    for t in range(4):
        for v in range(VIDEOS):
            out_ref[v, MINI * t : MINI * (t + 1)] = land[t, MINI * v : MINI * (v + 1)]


def per_device(
    tokens, prompt_ids, prompt_table, qkv_weight, out_weight, init_first, init_second, inner_rate
):
    vmem = pl.BlockSpec(memory_space=pltpu.VMEM)
    smem = pl.BlockSpec(memory_space=pltpu.SMEM)
    hbm = pl.BlockSpec(memory_space=pltpu.HBM)
    dma = pltpu.SemaphoreType.DMA
    return pl.pallas_call(
        kernel,
        out_shape=jax.ShapeDtypeStruct((VIDEOS, ROWS, 192), bf16),
        in_specs=[smem, smem] + [hbm] * 6,
        out_specs=vmem,
        scratch_shapes=[
            pltpu.VMEM((VIDEOS, ROWS, 3072), bf16),
            pltpu.VMEM((16, 3072), bf16),
            pltpu.VMEM((SEGS, VIDEOS * ROWS, 128), bf16),
            pltpu.VMEM((SEGS, 96, 384), bf16),
            pltpu.VMEM((VIDEOS * ROWS, 384), f32),
            pltpu.VMEM((8, 96, 128), bf16),
            pltpu.VMEM((SEGS, 96, 128), bf16),
            pltpu.VMEM((SEGS, 4, MINI, 128), f32),
            pltpu.VMEM((6, 8, MINI, 128), f32),
            pltpu.VMEM((64, 192), bf16),
            pltpu.VMEM((2048, 192), bf16),
            pltpu.VMEM((6, VIDEOS * MINI, 2048), bf16),
            pltpu.VMEM((6, VIDEOS * MINI, 192), bf16),
            pltpu.VMEM((4, VIDEOS * MINI, 192), bf16),
            pltpu.VMEM((HS, 256), bf16),
            pltpu.VMEM((HS, 256), bf16),
            pltpu.VMEM((ROWS, 256), bf16),
            pltpu.VMEM((2, 4, HS, 256), bf16),
            pltpu.VMEM((2, ROWS, HS), bf16),
            pltpu.VMEM((2, ROWS, HS), f32),
            pltpu.VMEM((2, 4, HS, MINI), f32),
            pltpu.VMEM((2, HS, ROWS), bf16),
            dma,
            dma,
            dma,
            dma((2,)),
            dma,
            dma,
            dma((SEGS, PARTS)),
            dma((8,)),
            dma((SEGS,)),
            dma,
            dma,
            dma,
            dma((6,)),
            dma((6,)),
            dma((6,)),
            dma((6,)),
            dma((6,)),
            dma,
            pltpu.SemaphoreType.REGULAR((4,)),
        ],
        compiler_params=pltpu.CompilerParams(
            collective_id=0, has_side_effects=True, vmem_limit_bytes=60 << 20
        ),
        name="chains",
    )(
        inner_rate,
        prompt_ids.T,
        tokens,
        prompt_table,
        jnp.transpose(qkv_weight, (1, 0, 2)),
        out_weight,
        init_first,
        init_second,
    )


def solution(mesh):
    return jax.shard_map(
        per_device,
        mesh=mesh,
        in_specs=(
            P(None, "seg", None),
            P(None, "seg"),
            P(),
            P("seg", None, "video"),
            P("seg", "video"),
            P("video", None, None),
            P("video", None, None),
            P("video"),
        ),
        out_specs=P(None, "seg", "video"),
        check_vma=False,
    )
```

```python
import jax
import jax.numpy as jnp
from jax import lax
from jax.experimental import pallas as pl
from jax.experimental.pallas import tpu as pltpu
from jax.sharding import PartitionSpec as P

HS = 64
MINI = 16
SEGS = 32
GROUPS = 16
VIDEOS = 2
ROWS = 64
EPS = 1e-6
OWN = 4
WORKERS = SEGS - 2 * OWN
PARTS = 1
PART = 96 // PARTS
C0 = 0.7978845608028654
C1 = C0 * 0.044715
f32 = jnp.float32
bf16 = jnp.bfloat16


def contract(a, b, da, db):
    return lax.dot_general(a, b, (((da,), (db,)), ((), ())), preferred_element_type=f32)


def nn(a, b):
    return contract(a, b, 1, 0)


def nt(a, b):
    return contract(a, b, 1, 1)


def tn(a, b):
    return contract(a, b, 0, 0)


def gelu_parts(x):
    x2 = x * x
    t = jnp.tanh(x * (C0 + C1 * x2))
    half = 0.5 * x
    return half + half * t, t, x2, half


def gelu_slope(t, x2, half):
    return (0.5 + 0.5 * t) + half * (1.0 - t * t) * (C0 + (3.0 * C1) * x2)


def remote(src, dst, send, recv, seg=None, video=None):
    where = {"seg": seg} if video is None else {"video": video}
    return pltpu.make_async_remote_copy(
        src_ref=src,
        dst_ref=dst,
        send_sem=send,
        recv_sem=recv,
        device_id=where,
        device_id_type=pl.DeviceIdType.MESH,
    )


def arrived(ref, sem):
    pltpu.make_async_copy(ref, ref, sem).wait()


def tell(sem, **where):
    pl.semaphore_signal(sem, inc=1, device_id=where, device_id_type=pl.DeviceIdType.MESH)


def kernel(
    rate_ref,
    ids_ref,
    tok_ref,
    table_ref,
    w_ref,
    ow_ref,
    first_ref,
    second_ref,
    out_ref,
    tok,
    table,
    xin,
    wall,
    acc,
    qmsg,
    qin,
    zst,
    zbuf,
    ow,
    owall,
    heads,
    res,
    land,
    first,
    second,
    grads,
    q_weights,
    p_query,
    p_target,
    p_across,
    p_turned,
    tok_sem,
    table_sem,
    w_sem,
    state_sem,
    ow_sem,
    w_send,
    w_recv,
    q_send,
    q_recv,
    o_send,
    o_recv,
    z_send,
    z_recv,
    h_send,
    h_recv,
    a_recv,
    r_send,
    r_recv,
    ring_sem,
):
    me = lax.axis_index("seg")
    vid = lax.axis_index("video")
    core = me % 2
    chip = me // 2
    x = chip // 4
    y = chip % 4
    is_owner = jnp.logical_or(me < OWN, me >= SEGS - OWN)
    is_worker = jnp.logical_not(is_owner)
    head = me % 2

    def at(xx, yy, cc):
        return ((xx % 4) * 4 + yy) * 2 + cc

    loads = [
        pltpu.make_async_copy(w_ref.at[j], wall.at[me, :, pl.ds(128 * j, 128)], w_sem) for j in range(3)
    ]
    loads.append(pltpu.make_async_copy(tok_ref, tok, tok_sem))
    loads.append(pltpu.make_async_copy(table_ref, table, table_sem))
    loads.append(pltpu.make_async_copy(first_ref.at[head], first, state_sem.at[0]))
    loads.append(pltpu.make_async_copy(second_ref.at[head], second, state_sem.at[1]))
    loads.append(pltpu.make_async_copy(ow_ref, ow, ow_sem))
    for load in loads:
        load.start()

    right, left, mate = at(x + 1, y, core), at(x + 3, y, core), at(x, y, 1 - core)
    y1 = y + 1 - 2 * (y % 2)
    y2 = (y + 2) % 4
    y3 = 3 - y
    ring = (vid // 8) * 8
    upper = ring + (vid + 1) % 8
    lower = ring + (vid + 7) % 8
    across = (vid + 8) % 16

    barrier = pltpu.get_barrier_semaphore()
    for target in (at(x, y1, core), at(x, y2, core), at(x, y3, core), right, left, mate):
        tell(barrier, seg=target)

    @pl.when(is_worker)
    def _():
        for target in (upper, lower, across):
            tell(barrier, video=target)

    lane = lax.broadcasted_iota(jnp.int32, (16, 16), 1)
    picks = [jnp.where(lane == ids_ref[0, v], 1.0, 0.0).astype(bf16) for v in range(VIDEOS)]

    def prepare(g, carry):
        span = pl.ds(pl.multiple_of(g * 384, 128), 384)
        for v in range(VIDEOS):
            bias = nn(picks[v], table[:, span])[0:1]
            part = (tok[v, :, span].astype(f32) + bias).astype(bf16)
            for i in range(4):
                xin[g * 4 + i, ROWS * v : ROWS * (v + 1), 0:96] = part[:, 96 * i : 96 * (i + 1)]
        return carry

    loads[3].wait()
    loads[4].wait()
    lax.fori_loop(0, 8, prepare, 0)
    acc[...] = jnp.zeros_like(acc)
    arrived(wall.at[me], w_sem)
    pl.semaphore_wait(barrier, jnp.where(is_worker, 9, 6))

    def y_of(k):
        return jnp.where(k == 0, y, jnp.where(k == 1, y1, jnp.where(k == 2, y2, y3)))

    def half_of(chunk, part):
        return wall.at[chunk, pl.ds(PART * part, PART)]

    def pass_on(chunk, part, target):
        block = half_of(chunk, part)
        remote(block, block, w_send, w_recv.at[chunk, part], seg=target).start()

    def start_lines(part):
        for target in (at(x, y1, core), at(x, y2, core), at(x, y3, core)):
            pass_on(me, part, target)

    start_lines(0)
    for part in range(PARTS):
        pass_on(me, part, right)
        pass_on(me, part, left)

    def landed(chunk, part):
        arrived(half_of(chunk, part), w_recv.at[chunk, part])

    def add(chunk):
        acc[...] += nn(xin[chunk, :, 0:96], wall[chunk])

    def y_step(part):
        def one(k, carry):
            chunk = at(x, y_of(k), core)
            landed(chunk, part)
            pass_on(chunk, part, right)
            pass_on(chunk, part, left)
            pass_on(chunk, part, mate)
            return carry

        one(1, 0)
        if part + 1 < PARTS:
            start_lines(part + 1)
        pass_on(me, part, mate)
        lax.fori_loop(2, 4, one, 0)

    def x_step(k, part):
        row = y_of(k)
        a = at(x + 3, row, core)
        b = at(x + 1, row, core)
        landed(a, part)
        to_right = (row + part) % 2 == 0

        @pl.when(to_right)
        def _():
            pass_on(a, part, right)

        pass_on(a, part, mate)
        landed(b, part)

        @pl.when(jnp.logical_not(to_right))
        def _():
            pass_on(b, part, left)

        pass_on(b, part, mate)

    def add_near(k, carry):
        add(at(x, y_of(k), core))
        add(at(x + 3, y_of(k), core))
        add(at(x + 1, y_of(k), core))
        return carry

    for part in range(PARTS):
        y_step(part)
        x_step(0, part)

        if part > 0:
            lax.fori_loop(1, 4, lambda k, c: (x_step(k, part - 1), c)[1], 0)
    lax.fori_loop(1, 4, lambda k, c: (x_step(k, PARTS - 1), c)[1], 0)
    lax.fori_loop(0, 4, add_near, 0)

    def other_add(chunk):
        for part in range(PARTS):
            landed(chunk, part)
        add(chunk)

    def far_step(k, carry):
        far = at(x + 2, y_of(k), core)
        for part in range(PARTS):
            landed(far, part)
            pass_on(far, part, mate)
        add(far)
        for i in (0, 1, 3):
            other_add(at(x + i, y_of(k), 1 - core))
        return carry

    lax.fori_loop(0, 4, far_step, 0)

    def last_step(k, carry):
        other_add(at(x + 2, y_of(k), 1 - core))
        return carry

    lax.fori_loop(0, 4, last_step, 0)

    low = lax.broadcasted_iota(jnp.int32, (1, 128), 1) < HS
    full = [acc[:, 128 * j : 128 * (j + 1)].astype(bf16).astype(f32) for j in range(3)]
    wanted = full[2] - full[1]
    mean_low = jnp.sum(jnp.where(low, wanted, 0.0), -1, keepdims=True) * (1.0 / HS)
    mean_high = jnp.sum(jnp.where(low, 0.0, wanted), -1, keepdims=True) * (1.0 / HS)
    full[2] = wanted - jnp.where(low, mean_low, mean_high)
    turned = [pltpu.roll(part, HS, 1) for part in full]
    for v in range(VIDEOS):
        q, k, val = [part[ROWS * v : ROWS * (v + 1)] for part in full]
        qt, kt, vt = [part[ROWS * v : ROWS * (v + 1)] for part in turned]
        for h in range(2):
            kq = jnp.where(low, k, qt) if h == 0 else jnp.where(low, kt, q)
            kq = kq.astype(bf16)
            for back in range(2):
                n = 4 * back + 2 * v + h
                order = [3, 2, 1, 0] if back else [0, 1, 2, 3]
                for t in range(4):
                    o = order[t]
                    qmsg[n, MINI * t : MINI * (t + 1)] = kq[MINI * o : MINI * (o + 1)]
                for t in range(2):
                    o, p = order[t], order[t + 2]
                    one, two = slice(MINI * o, MINI * (o + 1)), slice(MINI * p, MINI * (p + 1))
                    pair = jnp.where(low, val[one], vt[two]) if h == 0 else jnp.where(low, vt[one], val[two])
                    qmsg[n, ROWS + MINI * t : ROWS + MINI * (t + 1)] = pair.astype(bf16)

    def give(i):
        owner = jnp.where(i < 4, i, SEGS - 8 + i)

        @pl.when(owner == me)
        def _():
            pltpu.make_async_copy(qmsg.at[i], qin.at[me], q_recv.at[me]).start()

        @pl.when(owner != me)
        def _():
            remote(qmsg.at[i], qin.at[me], q_send.at[i], q_recv.at[me], seg=owner).start()

    def given(i):
        @pl.when(jnp.where(i < 4, i, SEGS - 8 + i) != me)
        def _():
            remote(qmsg.at[i], qin.at[me], q_send.at[i], q_recv.at[me], seg=right).wait_send()

    def give_soon(n, carry):
        give(jnp.where(me < 16, n, n + 4))
        return carry

    def give_later(n, carry):
        give(jnp.where(me < 16, n + 4, n))
        return carry

    def soon_given(n, carry):
        given(jnp.where(me < 16, n, n + 4))
        return carry

    def later_given(n, carry):
        given(jnp.where(me < 16, n + 4, n))
        return carry

    lax.fori_loop(0, 4, give_soon, 0)

    @pl.when(is_worker)
    def _():
        lax.fori_loop(0, 4, soon_given, 0)

    lax.fori_loop(0, 4, give_later, 0)

    loads[-1].wait()
    my_rows = pl.ds(pl.multiple_of(me * 64, 64), 64)

    def give_out_weight(i):
        target = OWN + (i + me) % WORKERS
        remote(ow, owall.at[my_rows], o_send, o_recv, seg=target).start()

    def piece_place(s, t):
        upper_half = jnp.where(s < 16, 0, 1)
        i = jnp.where(s < 16, 4 * s + t, 4 * (SEGS - 1 - s) + 3 - t)
        p = i % 12
        return OWN + 12 * upper_half + (p % 6) * 2 + p // 6, i // 12

    @pl.when(is_owner)
    def _():
        back = jnp.where(me < OWN, 0, 1)
        slot = jnp.where(me < OWN, me, me - (SEGS - 8))
        eta = rate_ref[head]
        loads[5].wait()
        loads[6].wait()

        def seg_of(j):
            return j + back * (SEGS - 1 - 2 * j)

        def give_answer(j, t):
            s = seg_of(j)
            target, place = piece_place(s, t + back * (3 - 2 * t))
            remote(zst.at[j, t], zbuf.at[place, slot], z_send, z_recv.at[place], seg=target).start()

        grads[...] = jnp.zeros_like(grads)
        row_block = lax.broadcasted_iota(jnp.int32, (ROWS, ROWS), 0) // MINI
        upto = row_block >= lax.broadcasted_iota(jnp.int32, (ROWS, ROWS), 1) // MINI

        def wait_for(j):
            s = seg_of(j)
            arrived(qin.at[s], q_recv.at[s])

        def lay_out(j, slot):
            s = seg_of(j)
            keys = qin[s, 0:ROWS, 0:HS]
            targets = jnp.concatenate([qin[s, ROWS:96, 0:HS], qin[s, ROWS:96, HS:128]], 0)
            p_query[slot] = qin[s, 0:ROWS, HS:128]
            p_turned[slot] = keys.T
            targets = targets.astype(f32)
            p_target[slot] = targets
            for t in range(4):
                p_across[slot, t] = targets[MINI * t : MINI * (t + 1)].T

        def query_hidden(slot, keys, layer_one, grad):
            queries = p_query[slot]
            cross = jnp.where(upto, -eta * nt(queries, keys), 0.0).astype(bf16)
            return gelu_parts(nn(queries, layer_one) + nn(cross, grad))[0].astype(bf16)

        def query_answers(slot, h, j, which):
            for t in which:
                rows = slice(MINI * t, MINI * (t + 1))
                c = nt(h[rows], q_weights[slot, t])
                rho = lax.rsqrt(jnp.mean(c * c, -1, keepdims=True) + EPS)
                zst[j, t, :, 0:HS] = p_query[slot, rows].astype(f32) + c * rho

        def answer_queries(slot, keys, layer_one, grad, j):
            query_answers(slot, query_hidden(slot, keys, layer_one, grad), j, range(4))

        def segment(j, pre, slot, begin=False, end=False):
            if not end:
                wait_for(j + 1)
            s, s_next = seg_of(j), seg_of(j if end else j + 1)
            keys = qin[s, 0:ROWS, 0:HS]
            targets = p_target[slot]
            targets_t = [p_across[slot, t] for t in range(4)]
            keys_ahead = jnp.concatenate([keys[MINI:], qin[s_next, 0:MINI, 0:HS]], 0)
            grads_before = grads[...]
            layer_one = first[...]
            if not begin:
                before = j - 1
                keys_before = qin[seg_of(before), 0:ROWS, 0:HS]
                layer_before = layer_one
                layer_one = (layer_one.astype(f32) - eta * nn(p_turned[1 - slot], grads_before)).astype(bf16)
                first[...] = layer_one
            base_k = nn(keys_ahead, layer_one)
            cross = -eta * nt(keys_ahead, keys)
            cross_b = cross.astype(bf16)
            layer_two = second[...].astype(f32)
            mu = jnp.mean(layer_two, 0, keepdims=True)
            centred = layer_two - mu
            ahead = [base_k[MINI * t : MINI * (t + 1)] for t in range(4)]
            done = []
            for t in range(4):
                rows = slice(MINI * t, MINI * (t + 1))
                h, th, x2, half = gelu_parts(pre)
                hb = h.astype(bf16)
                weights = centred.astype(bf16)
                target = targets[rows]
                c = nt(hb, weights)
                w = nn(target.astype(bf16), weights)
                u = nn(c.astype(bf16), weights)
                rho = lax.rsqrt(jnp.mean(c * c, -1, keepdims=True) + EPS)
                m = jnp.mean(target * c, -1, keepdims=True)
                r2 = rho * rho
                b = rho * (1.0 / MINI)
                a = (r2 * (1.0 / MINI)) * (EPS * r2 + rho * m)
                ct = nt(weights, hb)
                target_t = targets_t[t]
                rho_t = lax.rsqrt(jnp.sum(ct * ct, 0, keepdims=True) * (1.0 / HS) + EPS)
                m_t = jnp.sum(target_t * ct, 0, keepdims=True) * (1.0 / HS)
                r2_t = rho_t * rho_t
                b_t = rho_t * (eta / MINI)
                a_t = (r2_t * (-eta / MINI)) * (EPS * r2_t + rho_t * m_t)
                moved = centred + nn((a_t * ct + b_t * target_t).astype(bf16), hb)
                slope = gelu_slope(th, x2, half)
                grad = a * (u * slope) - b * (w * slope)
                grad_b = grad.astype(bf16)
                done.append(grad_b)
                sums = [ahead[t], None]
                for i in range(MINI):
                    col = cross[rows, MINI * t + i : MINI * t + i + 1]
                    term = jnp.broadcast_to(col, (MINI, 256)) * jnp.broadcast_to(grad[i : i + 1], (MINI, 256))
                    sums[i % 2] = term if sums[i % 2] is None else sums[i % 2] + term
                pre = sums[0] + sums[1]
                for r in range(t + 1, 4):
                    ahead[r] = ahead[r] + nn(cross_b[MINI * r : MINI * (r + 1), rows], grad_b)
                q_weights[slot, t] = moved.astype(bf16)
                centred = moved
                if t == 0 and not begin:
                    h_query = query_hidden(1 - slot, keys_before, layer_before, grads_before)
                if t == 0 and not begin:
                    query_answers(1 - slot, h_query, before, [0])
                if t == 1 and not begin:
                    query_answers(1 - slot, h_query, before, [1])
                if t == 2 and not begin:
                    query_answers(1 - slot, h_query, before, [2])
                if t == 3 and not begin:
                    query_answers(1 - slot, h_query, before, [3])
            grads[...] = jnp.concatenate(done, 0)
            second[...] = (centred + mu).astype(bf16)
            if not end:
                lay_out(j + 1, 1 - slot)
            if not begin:
                for t in range(4):
                    give_answer(before, t)
            return pre

        def send_out_weight(i, carry):
            give_out_weight(i)
            return carry

        lax.fori_loop(0, WORKERS, send_out_weight, 0)
        wait_for(0)
        pre = nn(qin[seg_of(0), 0:MINI, 0:HS], first[...])
        lay_out(0, 0)
        pre = segment(0, pre, 0, begin=True)

        def two_segments(i, pre):
            pre = segment(2 * i + 1, pre, 1)
            return segment(2 * i + 2, pre, 0)

        pre = lax.fori_loop(0, SEGS // 2 - 1, two_segments, pre)
        segment(SEGS - 1, pre, 1, end=True)
        s_last = seg_of(SEGS - 1)
        answer_queries(1, qin[s_last, 0:ROWS, 0:HS], first[...], grads[...], SEGS - 1)
        for t in range(4):
            give_answer(SEGS - 1, t)

    @pl.when(is_worker)
    def _():
        lax.fori_loop(0, 4, later_given, 0)

        def send_out_weight(i, carry):
            @pl.when(OWN + (i + me) % WORKERS != me)
            def _():
                give_out_weight(i)

            return carry

        lax.fori_loop(0, WORKERS, send_out_weight, 0)
        pltpu.make_async_copy(ow, owall.at[my_rows], o_recv).start()

        for k in range(3):
            tell(ring_sem.at[k], video=upper)
            tell(ring_sem.at[k], video=lower)
            pl.semaphore_wait(ring_sem.at[k], 2)
        tell(ring_sem.at[3], video=across)
        pl.semaphore_wait(ring_sem.at[3], 1)

        upper_half = jnp.where(me < 16, 0, 1)
        r = me - OWN - 12 * upper_half
        p = r // 2 + 6 * (r % 2)
        count = jnp.where(p < 4, 6, 5)
        mine = pl.ds(pl.multiple_of(vid * 128, 128), 128)
        theirs = pl.ds(pl.multiple_of(across * 128, 128), 128)

        def place_of(n):
            place = count - 1 - n
            i = 12 * place + p
            s = jnp.where(upper_half == 0, i // 4, SEGS - 1 - i // 4)
            t = jnp.where(upper_half == 0, i % 4, 3 - i % 4)
            return place, s, t

        def spread(place, columns):
            block = heads.at[place, :, columns]

            def one(d, carry):
                remote(
                    block, block, h_send.at[place], h_recv.at[place], video=ring + (vid + d) % 8
                ).start()
                return carry

            lax.fori_loop(1, 8, one, 0)

        def gather(n):
            place, _, _ = place_of(n)
            arrived(zbuf.at[place], z_recv.at[place])
            for v in range(VIDEOS):
                pair = [zbuf[place, 2 * v + h, :, 0:HS] + zbuf[place, 4 + 2 * v + h, :, 0:HS] for h in range(2)]
                heads[place, MINI * v : MINI * (v + 1), mine] = jnp.concatenate(pair, 1).astype(bf16)
            block = heads.at[place, :, mine]
            remote(block, block, h_send.at[place], a_recv.at[place], video=across).start()
            spread(place, mine)

        def relay(n):
            place, _, _ = place_of(n)
            arrived(heads.at[place, :, theirs], a_recv.at[place])
            spread(place, theirs)

        def finish(n):
            place, s, t = place_of(n)
            arrived(heads.at[place, :, pl.ds(0, 128 * 14)], h_recv.at[place])
            res[place] = nn(heads[place], owall[...]).astype(bf16)

            @pl.when(s == me)
            def _():
                pltpu.make_async_copy(res.at[place], land.at[t], r_recv).start()

            @pl.when(s != me)
            def _():
                remote(res.at[place], land.at[t], r_send.at[place], r_recv, seg=s).start()

        def piece(n, carry):
            relay(n - 2)
            gather(n)

            @pl.when(n >= 4)
            def _():
                finish(n - 4)

            return carry

        gather(0)
        gather(1)
        arrived(owall, o_recv)
        lax.fori_loop(2, count, piece, 0)
        relay(count - 2)
        finish(count - 4)
        finish(count - 3)
        relay(count - 1)
        finish(count - 2)
        finish(count - 1)

        def piece_sent(n, carry):
            i = 12 * n + p
            s = jnp.where(upper_half == 0, i // 4, SEGS - 1 - i // 4)
            arrived(heads.at[n, :, pl.ds(0, 128 * (GROUPS - 1))], h_send.at[n])

            @pl.when(s != me)
            def _():
                remote(res.at[n], land.at[0], r_send.at[n], r_recv, seg=s).wait_send()

            return carry

        lax.fori_loop(0, count, piece_sent, 0)
        arrived(owall.at[pl.ds(0, 64 * (WORKERS - 1))], o_send)
        loads[5].wait()
        loads[6].wait()

    @pl.when(is_owner)
    def _():
        lax.fori_loop(0, 4, soon_given, 0)
        lax.fori_loop(0, 4, later_given, 0)
        arrived(owall.at[pl.ds(0, 64 * WORKERS)], o_send)
        arrived(zst, z_send)

    arrived(wall.at[pl.ds(0, SEGS - 1)], w_send)

    arrived(land, r_recv)
    for t in range(4):
        for v in range(VIDEOS):
            out_ref[v, MINI * t : MINI * (t + 1)] = land[t, MINI * v : MINI * (v + 1)]


def per_device(
    tokens, prompt_ids, prompt_table, qkv_weight, out_weight, init_first, init_second, inner_rate
):
    vmem = pl.BlockSpec(memory_space=pltpu.VMEM)
    smem = pl.BlockSpec(memory_space=pltpu.SMEM)
    hbm = pl.BlockSpec(memory_space=pltpu.HBM)
    dma = pltpu.SemaphoreType.DMA
    return pl.pallas_call(
        kernel,
        out_shape=jax.ShapeDtypeStruct((VIDEOS, ROWS, 192), bf16),
        in_specs=[smem, smem] + [hbm] * 6,
        out_specs=vmem,
        scratch_shapes=[
            pltpu.VMEM((VIDEOS, ROWS, 3072), bf16),
            pltpu.VMEM((16, 3072), bf16),
            pltpu.VMEM((SEGS, VIDEOS * ROWS, 128), bf16),
            pltpu.VMEM((SEGS, 96, 384), bf16),
            pltpu.VMEM((VIDEOS * ROWS, 384), f32),
            pltpu.VMEM((8, 96, 128), bf16),
            pltpu.VMEM((SEGS, 96, 128), bf16),
            pltpu.VMEM((SEGS, 4, MINI, 128), f32),
            pltpu.VMEM((6, 8, MINI, 128), f32),
            pltpu.VMEM((64, 192), bf16),
            pltpu.VMEM((2048, 192), bf16),
            pltpu.VMEM((6, VIDEOS * MINI, 2048), bf16),
            pltpu.VMEM((6, VIDEOS * MINI, 192), bf16),
            pltpu.VMEM((4, VIDEOS * MINI, 192), bf16),
            pltpu.VMEM((HS, 256), bf16),
            pltpu.VMEM((HS, 256), bf16),
            pltpu.VMEM((ROWS, 256), bf16),
            pltpu.VMEM((2, 4, HS, 256), bf16),
            pltpu.VMEM((2, ROWS, HS), bf16),
            pltpu.VMEM((2, ROWS, HS), f32),
            pltpu.VMEM((2, 4, HS, MINI), f32),
            pltpu.VMEM((2, HS, ROWS), bf16),
            dma,
            dma,
            dma,
            dma((2,)),
            dma,
            dma,
            dma((SEGS, PARTS)),
            dma((8,)),
            dma((SEGS,)),
            dma,
            dma,
            dma,
            dma((6,)),
            dma((6,)),
            dma((6,)),
            dma((6,)),
            dma((6,)),
            dma,
            pltpu.SemaphoreType.REGULAR((4,)),
        ],
        compiler_params=pltpu.CompilerParams(
            collective_id=0, has_side_effects=True, vmem_limit_bytes=60 << 20
        ),
        name="chains",
    )(
        inner_rate,
        prompt_ids.T,
        tokens,
        prompt_table,
        jnp.transpose(qkv_weight, (1, 0, 2)),
        out_weight,
        init_first,
        init_second,
    )


def solution(mesh):
    return jax.shard_map(
        per_device,
        mesh=mesh,
        in_specs=(
            P(None, "seg", None),
            P(None, "seg"),
            P(),
            P("seg", None, "video"),
            P("seg", "video"),
            P("video", None, None),
            P("video", None, None),
            P("video"),
        ),
        out_specs=P(None, "seg", "video"),
        check_vma=False,
    )
```

```python
import jax
import jax.numpy as jnp
from jax import lax
from jax.experimental import pallas as pl
from jax.experimental.pallas import tpu as pltpu
from jax.sharding import PartitionSpec as P

HS = 64
MINI = 16
SEGS = 32
GROUPS = 16
VIDEOS = 2
ROWS = 64
EPS = 1e-6
OWN = 4
WORKERS = SEGS - 2 * OWN
PARTS = 1
PART = 96 // PARTS
C0 = 0.7978845608028654
C1 = C0 * 0.044715
f32 = jnp.float32
bf16 = jnp.bfloat16


def contract(a, b, da, db):
    return lax.dot_general(a, b, (((da,), (db,)), ((), ())), preferred_element_type=f32)


def nn(a, b):
    return contract(a, b, 1, 0)


def nt(a, b):
    return contract(a, b, 1, 1)


def tn(a, b):
    return contract(a, b, 0, 0)


def gelu_parts(x):
    x2 = x * x
    t = jnp.tanh(x * (C0 + C1 * x2))
    half = 0.5 * x
    return half + half * t, t, x2, half


def gelu_slope(t, x2, half):
    return (0.5 + 0.5 * t) + half * (1.0 - t * t) * (C0 + (3.0 * C1) * x2)


def remote(src, dst, send, recv, **where):
    return pltpu.make_async_remote_copy(
        src_ref=src,
        dst_ref=dst,
        send_sem=send,
        recv_sem=recv,
        device_id=where,
        device_id_type=pl.DeviceIdType.MESH,
    )


def arrived(ref, sem):
    pltpu.make_async_copy(ref, ref, sem).wait()


def tell(sem, **where):
    pl.semaphore_signal(sem, inc=1, device_id=where, device_id_type=pl.DeviceIdType.MESH)


def kernel(
    rate_ref,
    ids_ref,
    tok_ref,
    table_ref,
    w_ref,
    ow_ref,
    first_ref,
    second_ref,
    out_ref,
    tok,
    table,
    xin,
    wall,
    acc,
    qmsg,
    qin,
    zst,
    zbuf,
    zfar,
    ow,
    owall,
    heads,
    res,
    land,
    first,
    second,
    grads,
    q_weights,
    p_query,
    p_target,
    p_across,
    p_turned,
    tok_sem,
    table_sem,
    w_sem,
    state_sem,
    ow_sem,
    w_send,
    w_recv,
    q_send,
    q_recv,
    o_send,
    o_recv,
    m_recv,
    z_send,
    z_recv,
    h_send,
    h_recv,
    a_recv,
    r_send,
    r_recv,
    f_send,
    f_recv,
    ring_sem,
    pair_sem,
):
    me = lax.axis_index("seg")
    vid = lax.axis_index("video")
    core = me % 2
    chip = me // 2
    x = chip // 4
    y = chip % 4
    is_owner = jnp.logical_or(me < OWN, me >= SEGS - OWN)
    is_worker = jnp.logical_not(is_owner)
    head = me % 2

    def at(xx, yy, cc):
        return ((xx % 4) * 4 + yy) * 2 + cc

    loads = [
        pltpu.make_async_copy(w_ref.at[j], wall.at[me, :, pl.ds(128 * j, 128)], w_sem) for j in range(3)
    ]
    loads.append(pltpu.make_async_copy(tok_ref, tok, tok_sem))
    loads.append(pltpu.make_async_copy(table_ref, table, table_sem))
    loads.append(pltpu.make_async_copy(first_ref.at[head], first, state_sem.at[0]))
    loads.append(pltpu.make_async_copy(second_ref.at[head], second, state_sem.at[1]))
    loads.append(pltpu.make_async_copy(ow_ref, ow, ow_sem))
    for load in loads:
        load.start()

    right, left, mate = at(x + 1, y, core), at(x + 3, y, core), at(x, y, 1 - core)
    y1 = y + 1 - 2 * (y % 2)
    y2 = (y + 2) % 4
    y3 = 3 - y
    ring = (vid // 8) * 8
    upper = ring + (vid + 1) % 8
    lower = ring + (vid + 7) % 8
    across = (vid + 8) % 16

    barrier = pltpu.get_barrier_semaphore()
    for target in (at(x, y1, core), at(x, y2, core), at(x, y3, core), right, left, mate):
        tell(barrier, seg=target)

    tell(barrier, video=across)

    @pl.when(is_worker)
    def _():
        for target in (upper, lower):
            tell(barrier, video=target)

    lane = lax.broadcasted_iota(jnp.int32, (16, 16), 1)
    picks = [jnp.where(lane == ids_ref[0, v], 1.0, 0.0).astype(bf16) for v in range(VIDEOS)]

    def prepare(g, carry):
        span = pl.ds(pl.multiple_of(g * 384, 128), 384)
        for v in range(VIDEOS):
            bias = nn(picks[v], table[:, span])[0:1]
            part = (tok[v, :, span].astype(f32) + bias).astype(bf16)
            for i in range(4):
                xin[g * 4 + i, ROWS * v : ROWS * (v + 1), 0:96] = part[:, 96 * i : 96 * (i + 1)]
        return carry

    loads[3].wait()
    loads[4].wait()
    lax.fori_loop(0, 8, prepare, 0)
    acc[...] = jnp.zeros_like(acc)
    arrived(wall.at[me], w_sem)
    pl.semaphore_wait(barrier, jnp.where(is_worker, 9, 7))

    def y_of(k):
        return jnp.where(k == 0, y, jnp.where(k == 1, y1, jnp.where(k == 2, y2, y3)))

    def half_of(chunk, part):
        return wall.at[chunk, pl.ds(PART * part, PART)]

    def pass_on(chunk, part, target):
        block = half_of(chunk, part)
        remote(block, block, w_send, w_recv.at[chunk, part], seg=target).start()

    def start_lines(part):
        for target in (at(x, y1, core), at(x, y2, core), at(x, y3, core)):
            pass_on(me, part, target)

    start_lines(0)
    for part in range(PARTS):
        pass_on(me, part, right)
        pass_on(me, part, left)

    def landed(chunk, part):
        arrived(half_of(chunk, part), w_recv.at[chunk, part])

    def add(chunk):
        acc[...] += nn(xin[chunk, :, 0:96], wall[chunk])

    def y_step(part):
        def one(k, carry):
            chunk = at(x, y_of(k), core)
            landed(chunk, part)
            pass_on(chunk, part, right)
            pass_on(chunk, part, left)
            pass_on(chunk, part, mate)
            return carry

        one(1, 0)
        if part + 1 < PARTS:
            start_lines(part + 1)
        pass_on(me, part, mate)
        lax.fori_loop(2, 4, one, 0)

    def x_step(k, part):
        row = y_of(k)
        a = at(x + 3, row, core)
        b = at(x + 1, row, core)
        landed(a, part)
        to_right = (row + part) % 2 == 0

        @pl.when(to_right)
        def _():
            pass_on(a, part, right)

        pass_on(a, part, mate)
        landed(b, part)

        @pl.when(jnp.logical_not(to_right))
        def _():
            pass_on(b, part, left)

        pass_on(b, part, mate)

    def add_near(k, carry):
        add(at(x, y_of(k), core))
        add(at(x + 3, y_of(k), core))
        add(at(x + 1, y_of(k), core))
        return carry

    for part in range(PARTS):
        y_step(part)
        x_step(0, part)

        if part > 0:
            lax.fori_loop(1, 4, lambda k, c: (x_step(k, part - 1), c)[1], 0)
    lax.fori_loop(1, 4, lambda k, c: (x_step(k, PARTS - 1), c)[1], 0)
    lax.fori_loop(0, 4, add_near, 0)

    def other_add(chunk):
        for part in range(PARTS):
            landed(chunk, part)
        add(chunk)

    def far_step(k, carry):
        far = at(x + 2, y_of(k), core)
        for part in range(PARTS):
            landed(far, part)
            pass_on(far, part, mate)
        add(far)
        for i in (0, 1, 3):
            other_add(at(x + i, y_of(k), 1 - core))
        return carry

    lax.fori_loop(0, 4, far_step, 0)

    def last_step(k, carry):
        other_add(at(x + 2, y_of(k), 1 - core))
        return carry

    lax.fori_loop(0, 4, last_step, 0)

    low = lax.broadcasted_iota(jnp.int32, (1, 128), 1) < HS
    full = [acc[:, 128 * j : 128 * (j + 1)].astype(bf16).astype(f32) for j in range(3)]
    wanted = full[2] - full[1]
    mean_low = jnp.sum(jnp.where(low, wanted, 0.0), -1, keepdims=True) * (1.0 / HS)
    mean_high = jnp.sum(jnp.where(low, 0.0, wanted), -1, keepdims=True) * (1.0 / HS)
    full[2] = wanted - jnp.where(low, mean_low, mean_high)
    turned = [pltpu.roll(part, HS, 1) for part in full]
    for v in range(VIDEOS):
        q, k, val = [part[ROWS * v : ROWS * (v + 1)] for part in full]
        qt, kt, vt = [part[ROWS * v : ROWS * (v + 1)] for part in turned]
        for h in range(2):
            kq = jnp.where(low, k, qt) if h == 0 else jnp.where(low, kt, q)
            kq = kq.astype(bf16)
            for back in range(2):
                n = 4 * back + 2 * v + h
                order = [3, 2, 1, 0] if back else [0, 1, 2, 3]
                for t in range(4):
                    o = order[t]
                    qmsg[n, MINI * t : MINI * (t + 1)] = kq[MINI * o : MINI * (o + 1)]
                for t in range(2):
                    o, p = order[t], order[t + 2]
                    one, two = slice(MINI * o, MINI * (o + 1)), slice(MINI * p, MINI * (p + 1))
                    pair = jnp.where(low, val[one], vt[two]) if h == 0 else jnp.where(low, vt[one], val[two])
                    qmsg[n, ROWS + MINI * t : ROWS + MINI * (t + 1)] = pair.astype(bf16)

    def give(i):
        owner = jnp.where(i < 4, i, SEGS - 8 + i)

        @pl.when(owner == me)
        def _():
            pltpu.make_async_copy(qmsg.at[i], qin.at[me], q_recv.at[me]).start()

        @pl.when(owner != me)
        def _():
            remote(qmsg.at[i], qin.at[me], q_send.at[i], q_recv.at[me], seg=owner).start()

    def given(i):
        @pl.when(jnp.where(i < 4, i, SEGS - 8 + i) != me)
        def _():
            remote(qmsg.at[i], qin.at[me], q_send.at[i], q_recv.at[me], seg=right).wait_send()

    def give_soon(n, carry):
        give(jnp.where(me < 16, n, n + 4))
        return carry

    def give_later(n, carry):
        give(jnp.where(me < 16, n + 4, n))
        return carry

    def soon_given(n, carry):
        given(jnp.where(me < 16, n, n + 4))
        return carry

    def later_given(n, carry):
        given(jnp.where(me < 16, n + 4, n))
        return carry

    lax.fori_loop(0, 4, give_soon, 0)

    @pl.when(is_worker)
    def _():
        lax.fori_loop(0, 4, soon_given, 0)

    lax.fori_loop(0, 4, give_later, 0)

    loads[-1].wait()
    my_rows = pl.ds(pl.multiple_of(me * 64, 64), 64)

    def give_out_weight(i):
        target = OWN + 2 * ((i + chip) % (WORKERS // 2)) + core
        remote(ow, owall.at[my_rows], o_send, o_recv, seg=target).start()

    def piece_place(s, t):
        upper_half = jnp.where(s < 16, 0, 1)
        i = jnp.where(s < 16, 4 * s + t, 4 * (SEGS - 1 - s) + 3 - t)
        p = i % 12
        return OWN + 12 * upper_half + (p % 6) * 2 + p // 6, i // 12

    @pl.when(is_owner)
    def _():
        back = jnp.where(me < OWN, 0, 1)
        slot = jnp.where(me < OWN, me, me - (SEGS - 8))
        eta = rate_ref[head]
        loads[5].wait()
        loads[6].wait()

        def seg_of(j):
            return j + back * (SEGS - 1 - 2 * j)

        def give_answer(j, t):
            s = seg_of(j)
            target, place = piece_place(s, t + back * (3 - 2 * t))
            remote(zst.at[j, t], zbuf.at[place, slot], z_send, z_recv.at[place], seg=target).start()

        def give_across(j, t):
            target, _ = piece_place(seg_of(j), t + back * (3 - 2 * t))
            remote(zst.at[j, t], zfar.at[slot], f_send, f_recv, seg=target, video=across).start()

        tell(pair_sem, video=across)
        grads[...] = jnp.zeros_like(grads)
        row_block = lax.broadcasted_iota(jnp.int32, (ROWS, ROWS), 0) // MINI
        upto = row_block >= lax.broadcasted_iota(jnp.int32, (ROWS, ROWS), 1) // MINI

        def wait_for(j):
            s = seg_of(j)
            arrived(qin.at[s], q_recv.at[s])

        def lay_out(j, slot):
            s = seg_of(j)
            keys = qin[s, 0:ROWS, 0:HS]
            targets = jnp.concatenate([qin[s, ROWS:96, 0:HS], qin[s, ROWS:96, HS:128]], 0)
            p_query[slot] = qin[s, 0:ROWS, HS:128]
            p_turned[slot] = keys.T
            targets = targets.astype(f32)
            p_target[slot] = targets
            for t in range(4):
                p_across[slot, t] = targets[MINI * t : MINI * (t + 1)].T

        def query_hidden(slot, keys, layer_one, grad):
            queries = p_query[slot]
            cross = jnp.where(upto, -eta * nt(queries, keys), 0.0).astype(bf16)
            return gelu_parts(nn(queries, layer_one) + nn(cross, grad))[0].astype(bf16)

        def query_answers(slot, h, j, which):
            for t in which:
                rows = slice(MINI * t, MINI * (t + 1))
                c = nt(h[rows], q_weights[slot, t])
                rho = lax.rsqrt(jnp.mean(c * c, -1, keepdims=True) + EPS)
                zst[j, t, :, 0:HS] = (p_query[slot, rows].astype(f32) + c * rho).astype(bf16)

        def answer_queries(slot, keys, layer_one, grad, j):
            query_answers(slot, query_hidden(slot, keys, layer_one, grad), j, range(4))

        def segment(j, pre, slot, begin=False, end=False):
            if not end:
                wait_for(j + 1)
            s, s_next = seg_of(j), seg_of(j if end else j + 1)
            keys = qin[s, 0:ROWS, 0:HS]
            targets = p_target[slot]
            targets_t = [p_across[slot, t] for t in range(4)]
            keys_ahead = jnp.concatenate([keys[MINI:], qin[s_next, 0:MINI, 0:HS]], 0)
            grads_before = grads[...]
            layer_one = first[...]
            if not begin:
                before = j - 1
                keys_before = qin[seg_of(before), 0:ROWS, 0:HS]
                layer_before = layer_one
                layer_one = (layer_one.astype(f32) - eta * nn(p_turned[1 - slot], grads_before)).astype(bf16)
                first[...] = layer_one
            base_k = nn(keys_ahead, layer_one)
            cross = -eta * nt(keys_ahead, keys)
            cross_b = cross.astype(bf16)
            layer_two = second[...].astype(f32)
            mu = jnp.mean(layer_two, 0, keepdims=True)
            centred = layer_two - mu
            ahead = [base_k[MINI * t : MINI * (t + 1)] for t in range(4)]
            done = []
            for t in range(4):
                rows = slice(MINI * t, MINI * (t + 1))
                h, th, x2, half = gelu_parts(pre)
                hb = h.astype(bf16)
                weights = centred.astype(bf16)
                target = targets[rows]
                c = nt(hb, weights)
                w = nn(target.astype(bf16), weights)
                u = nn(c.astype(bf16), weights)
                rho = lax.rsqrt(jnp.mean(c * c, -1, keepdims=True) + EPS)
                m = jnp.mean(target * c, -1, keepdims=True)
                r2 = rho * rho
                b = rho * (1.0 / MINI)
                a = (r2 * (1.0 / MINI)) * (EPS * r2 + rho * m)
                ct = nt(weights, hb)
                target_t = targets_t[t]
                rho_t = lax.rsqrt(jnp.sum(ct * ct, 0, keepdims=True) * (1.0 / HS) + EPS)
                m_t = jnp.sum(target_t * ct, 0, keepdims=True) * (1.0 / HS)
                r2_t = rho_t * rho_t
                b_t = rho_t * (eta / MINI)
                a_t = (r2_t * (-eta / MINI)) * (EPS * r2_t + rho_t * m_t)
                moved = centred + nn((a_t * ct + b_t * target_t).astype(bf16), hb)
                slope = gelu_slope(th, x2, half)
                grad = a * (u * slope) - b * (w * slope)
                grad_b = grad.astype(bf16)
                done.append(grad_b)
                sums = [ahead[t], None]
                for i in range(MINI):
                    col = cross[rows, MINI * t + i : MINI * t + i + 1]
                    term = jnp.broadcast_to(col, (MINI, 256)) * jnp.broadcast_to(grad[i : i + 1], (MINI, 256))
                    sums[i % 2] = term if sums[i % 2] is None else sums[i % 2] + term
                pre = sums[0] + sums[1]
                for r in range(t + 1, 4):
                    ahead[r] = ahead[r] + nn(cross_b[MINI * r : MINI * (r + 1), rows], grad_b)
                q_weights[slot, t] = moved.astype(bf16)
                centred = moved
                if t == 0 and not begin:
                    h_query = query_hidden(1 - slot, keys_before, layer_before, grads_before)
                if t == 0 and not begin:
                    query_answers(1 - slot, h_query, before, [0])
                if t == 1 and not begin:
                    query_answers(1 - slot, h_query, before, [1])
                if t == 2 and not begin:
                    query_answers(1 - slot, h_query, before, [2])
                if t == 3 and not begin:
                    query_answers(1 - slot, h_query, before, [3])
            grads[...] = jnp.concatenate(done, 0)
            second[...] = (centred + mu).astype(bf16)
            if not end:
                lay_out(j + 1, 1 - slot)
            if not begin:
                for t in range(4):
                    give_answer(before, t)
            if end:
                for t in range(4):
                    give_across(before, t)
            return pre

        def send_out_weight(i, carry):
            give_out_weight(i)
            return carry

        lax.fori_loop(0, WORKERS // 2, send_out_weight, 0)
        wait_for(0)
        pre = nn(qin[seg_of(0), 0:MINI, 0:HS], first[...])
        lay_out(0, 0)
        pre = segment(0, pre, 0, begin=True)

        def two_segments(i, pre):
            pre = segment(2 * i + 1, pre, 1)
            pre = segment(2 * i + 2, pre, 0)

            @pl.when(i == 1)
            def _():
                pl.semaphore_wait(pair_sem, 1)
                for j in range(3):
                    for t in range(4):
                        give_across(j, t)

            @pl.when(i == SEGS // 2 - 2)
            def _():
                for t in range(4):
                    give_across(SEGS - 3, t)

            return pre

        pre = lax.fori_loop(0, SEGS // 2 - 1, two_segments, pre)
        segment(SEGS - 1, pre, 1, end=True)
        s_last = seg_of(SEGS - 1)
        answer_queries(1, qin[s_last, 0:ROWS, 0:HS], first[...], grads[...], SEGS - 1)
        for t in range(4):
            give_answer(SEGS - 1, t)
            give_across(SEGS - 1, t)

    @pl.when(is_worker)
    def _():
        lax.fori_loop(0, 4, later_given, 0)

        def send_out_weight(i, carry):
            @pl.when(OWN + 2 * ((i + chip) % (WORKERS // 2)) + core != me)
            def _():
                give_out_weight(i)

            return carry

        lax.fori_loop(0, WORKERS // 2, send_out_weight, 0)
        pltpu.make_async_copy(ow, owall.at[my_rows], o_recv).start()

        for k in range(3):
            tell(ring_sem.at[k], video=upper)
            tell(ring_sem.at[k], video=lower)
            pl.semaphore_wait(ring_sem.at[k], 2)
        tell(ring_sem.at[3], video=across)
        pl.semaphore_wait(ring_sem.at[3], 1)

        upper_half = jnp.where(me < 16, 0, 1)
        r = me - OWN - 12 * upper_half
        p = r // 2 + 6 * (r % 2)
        count = jnp.where(p < 4, 6, 5)
        mine = pl.ds(pl.multiple_of(vid * 128, 128), 128)
        theirs = pl.ds(pl.multiple_of(across * 128, 128), 128)

        def place_of(n):
            place = count - 1 - n
            i = 12 * place + p
            s = jnp.where(upper_half == 0, i // 4, SEGS - 1 - i // 4)
            t = jnp.where(upper_half == 0, i % 4, 3 - i % 4)
            return place, s, t

        def spread(place, columns):
            block = heads.at[place, :, columns]

            def one(d, carry):
                remote(
                    block, block, h_send.at[place], h_recv.at[place], video=ring + (vid + d) % 8
                ).start()
                return carry

            lax.fori_loop(1, 8, one, 0)

        def write_heads(place, columns, answers):
            for v in range(VIDEOS):
                both = [answers[i].astype(f32) for i in (2 * v, 2 * v + 1, 2 * v + 4, 2 * v + 5)]
                pair = [both[h] + both[2 + h] for h in range(2)]
                heads[place, MINI * v : MINI * (v + 1), columns] = jnp.concatenate(pair, 1).astype(bf16)

        def gather_last():
            arrived(zbuf.at[0], z_recv.at[0])
            write_heads(0, mine, [zbuf[0, i, :, 0:HS] for i in range(8)])
            spread(0, mine)
            arrived(zfar, f_recv)
            write_heads(0, theirs, [zfar[i, :, 0:HS] for i in range(8)])
            spread(0, theirs)

        def gather(n):
            place, _, _ = place_of(n)
            arrived(zbuf.at[place], z_recv.at[place])
            write_heads(place, mine, [zbuf[place, i, :, 0:HS] for i in range(8)])
            block = heads.at[place, :, mine]
            remote(block, block, h_send.at[place], a_recv.at[place], video=across).start()
            spread(place, mine)

        def relay(n):
            place, _, _ = place_of(n)
            arrived(heads.at[place, :, theirs], a_recv.at[place])
            spread(place, theirs)

        def finish(n):
            place, s, t = place_of(n)
            arrived(heads.at[place, :, pl.ds(0, 128 * 14)], h_recv.at[place])
            res[place] = nn(heads[place], owall[...]).astype(bf16)

            @pl.when(s == me)
            def _():
                pltpu.make_async_copy(res.at[place], land.at[t], r_recv).start()

            @pl.when(s != me)
            def _():
                remote(res.at[place], land.at[t], r_send.at[place], r_recv, seg=s).start()

        def piece(n, carry):
            relay(n - 2)
            gather(n)

            @pl.when(n >= 4)
            def _():
                finish(n - 4)

            return carry

        half_of_all = owall.at[pl.ds(0, 1024)]
        arrived(half_of_all, o_recv)

        def share(i, carry):
            block = owall.at[pl.ds(pl.multiple_of((2 * i + core) * 64, 64), 64)]
            remote(block, block, o_send, m_recv, seg=mate).start()
            return carry

        lax.fori_loop(0, 16, share, 0)
        gather(0)
        gather(1)
        arrived(half_of_all, m_recv)
        lax.fori_loop(2, count - 1, piece, 0)
        relay(count - 3)
        finish(count - 5)
        relay(count - 2)
        finish(count - 4)
        gather_last()
        finish(count - 3)
        finish(count - 2)
        finish(count - 1)

        def piece_sent(n, carry):
            i = 12 * n + p
            s = jnp.where(upper_half == 0, i // 4, SEGS - 1 - i // 4)

            @pl.when(n == 0)
            def _():
                arrived(heads.at[n, :, pl.ds(0, 128 * 14)], h_send.at[n])

            @pl.when(n > 0)
            def _():
                arrived(heads.at[n, :, pl.ds(0, 128 * 15)], h_send.at[n])

            @pl.when(s != me)
            def _():
                remote(res.at[n], land.at[0], r_send.at[n], r_recv, seg=s).wait_send()

            return carry

        lax.fori_loop(0, count, piece_sent, 0)
        arrived(owall.at[pl.ds(0, 64 * (WORKERS // 2 - 1 + 16))], o_send)
        loads[5].wait()
        loads[6].wait()

    @pl.when(is_owner)
    def _():
        lax.fori_loop(0, 4, soon_given, 0)
        lax.fori_loop(0, 4, later_given, 0)
        arrived(owall.at[pl.ds(0, 64 * (WORKERS // 2))], o_send)
        arrived(zst, z_send)
        arrived(zst.at[pl.ds(0, 6)], f_send)

    arrived(wall.at[pl.ds(0, SEGS - 1)], w_send)

    arrived(land, r_recv)
    for t in range(4):
        for v in range(VIDEOS):
            out_ref[v, MINI * t : MINI * (t + 1)] = land[t, MINI * v : MINI * (v + 1)]


def per_device(
    tokens, prompt_ids, prompt_table, qkv_weight, out_weight, init_first, init_second, inner_rate
):
    vmem = pl.BlockSpec(memory_space=pltpu.VMEM)
    smem = pl.BlockSpec(memory_space=pltpu.SMEM)
    hbm = pl.BlockSpec(memory_space=pltpu.HBM)
    dma = pltpu.SemaphoreType.DMA
    return pl.pallas_call(
        kernel,
        out_shape=jax.ShapeDtypeStruct((VIDEOS, ROWS, 192), bf16),
        in_specs=[smem, smem] + [hbm] * 6,
        out_specs=vmem,
        scratch_shapes=[
            pltpu.VMEM((VIDEOS, ROWS, 3072), bf16),
            pltpu.VMEM((16, 3072), bf16),
            pltpu.VMEM((SEGS, VIDEOS * ROWS, 128), bf16),
            pltpu.VMEM((SEGS, 96, 384), bf16),
            pltpu.VMEM((VIDEOS * ROWS, 384), f32),
            pltpu.VMEM((8, 96, 128), bf16),
            pltpu.VMEM((SEGS, 96, 128), bf16),
            pltpu.VMEM((SEGS, 4, MINI, 128), bf16),
            pltpu.VMEM((6, 8, MINI, 128), bf16),
            pltpu.VMEM((8, MINI, 128), bf16),
            pltpu.VMEM((64, 192), bf16),
            pltpu.VMEM((2048, 192), bf16),
            pltpu.VMEM((6, VIDEOS * MINI, 2048), bf16),
            pltpu.VMEM((6, VIDEOS * MINI, 192), bf16),
            pltpu.VMEM((4, VIDEOS * MINI, 192), bf16),
            pltpu.VMEM((HS, 256), bf16),
            pltpu.VMEM((HS, 256), bf16),
            pltpu.VMEM((ROWS, 256), bf16),
            pltpu.VMEM((2, 4, HS, 256), bf16),
            pltpu.VMEM((2, ROWS, HS), bf16),
            pltpu.VMEM((2, ROWS, HS), f32),
            pltpu.VMEM((2, 4, HS, MINI), f32),
            pltpu.VMEM((2, HS, ROWS), bf16),
            dma,
            dma,
            dma,
            dma((2,)),
            dma,
            dma,
            dma((SEGS, PARTS)),
            dma((8,)),
            dma((SEGS,)),
            dma,
            dma,
            dma,
            dma,
            dma((6,)),
            dma((6,)),
            dma((6,)),
            dma((6,)),
            dma((6,)),
            dma,
            dma,
            dma,
            pltpu.SemaphoreType.REGULAR((4,)),
            pltpu.SemaphoreType.REGULAR,
        ],
        compiler_params=pltpu.CompilerParams(
            collective_id=0, has_side_effects=True, vmem_limit_bytes=60 << 20
        ),
        name="chains",
    )(
        inner_rate,
        prompt_ids.T,
        tokens,
        prompt_table,
        jnp.transpose(qkv_weight, (1, 0, 2)),
        out_weight,
        init_first,
        init_second,
    )


def solution(mesh):
    return jax.shard_map(
        per_device,
        mesh=mesh,
        in_specs=(
            P(None, "seg", None),
            P(None, "seg"),
            P(),
            P("seg", None, "video"),
            P("seg", "video"),
            P("video", None, None),
            P("video", None, None),
            P("video"),
        ),
        out_specs=P(None, "seg", "video"),
        check_vma=False,
    )
```

```python
import jax
import jax.numpy as jnp
from jax import lax
from jax.experimental import pallas as pl
from jax.experimental.pallas import tpu as pltpu
from jax.sharding import PartitionSpec as P

HS = 64
MINI = 16
SEGS = 32
GROUPS = 16
VIDEOS = 2
ROWS = 64
EPS = 1e-6
OWN = 4
WORKERS = SEGS - 2 * OWN
PARTS = 1
PART = 96 // PARTS
C0 = 0.7978845608028654
C1 = C0 * 0.044715
f32 = jnp.float32
bf16 = jnp.bfloat16


def contract(a, b, da, db):
    return lax.dot_general(a, b, (((da,), (db,)), ((), ())), preferred_element_type=f32)


def nn(a, b):
    return contract(a, b, 1, 0)


def nt(a, b):
    return contract(a, b, 1, 1)


def tn(a, b):
    return contract(a, b, 0, 0)


def gelu_parts(x):
    x2 = x * x
    t = jnp.tanh(x * (C0 + C1 * x2))
    half = 0.5 * x
    return half + half * t, t, x2, half


def gelu_slope(t, x2, half):
    return (0.5 + 0.5 * t) + half * (1.0 - t * t) * (C0 + (3.0 * C1) * x2)


def remote(src, dst, send, recv, **where):
    return pltpu.make_async_remote_copy(
        src_ref=src,
        dst_ref=dst,
        send_sem=send,
        recv_sem=recv,
        device_id=where,
        device_id_type=pl.DeviceIdType.MESH,
    )


def arrived(ref, sem):
    pltpu.make_async_copy(ref, ref, sem).wait()


def tell(sem, **where):
    pl.semaphore_signal(sem, inc=1, device_id=where, device_id_type=pl.DeviceIdType.MESH)


def kernel(
    rate_ref,
    ids_ref,
    tok_ref,
    table_ref,
    w_ref,
    ow_ref,
    first_ref,
    second_ref,
    out_ref,
    tok,
    table,
    xin,
    wall,
    acc,
    qmsg,
    qin,
    zst,
    zbuf,
    zfar,
    ow,
    owall,
    heads,
    res,
    land,
    first,
    second,
    grads,
    q_weights,
    p_query,
    p_target,
    p_across,
    p_turned,
    tok_sem,
    table_sem,
    w_sem,
    state_sem,
    ow_sem,
    w_send,
    w_recv,
    q_send,
    q_recv,
    o_send,
    o_recv,
    m_recv,
    z_send,
    z_recv,
    h_send,
    h_recv,
    a_recv,
    r_send,
    r_recv,
    f_send,
    f_recv,
    ring_sem,
    pair_sem,
):
    me = lax.axis_index("seg")
    vid = lax.axis_index("video")
    core = me % 2
    chip = me // 2
    x = chip // 4
    y = chip % 4
    is_owner = jnp.logical_or(me < OWN, me >= SEGS - OWN)
    is_worker = jnp.logical_not(is_owner)
    head = me % 2

    def at(xx, yy, cc):
        return ((xx % 4) * 4 + yy) * 2 + cc

    loads = [
        pltpu.make_async_copy(w_ref.at[j], wall.at[me, :, pl.ds(128 * j, 128)], w_sem) for j in range(3)
    ]
    loads.append(pltpu.make_async_copy(tok_ref, tok, tok_sem))
    loads.append(pltpu.make_async_copy(table_ref, table, table_sem))
    loads.append(pltpu.make_async_copy(first_ref.at[head], first, state_sem.at[0]))
    loads.append(pltpu.make_async_copy(second_ref.at[head], second, state_sem.at[1]))
    loads.append(pltpu.make_async_copy(ow_ref, ow, ow_sem))
    for load in loads:
        load.start()

    right, left, mate = at(x + 1, y, core), at(x + 3, y, core), at(x, y, 1 - core)
    y1 = y + 1 - 2 * (y % 2)
    y2 = (y + 2) % 4
    y3 = 3 - y
    ring = (vid // 8) * 8
    upper = ring + (vid + 1) % 8
    lower = ring + (vid + 7) % 8
    across = (vid + 8) % 16

    barrier = pltpu.get_barrier_semaphore()
    for target in (at(x, y1, core), at(x, y2, core), at(x, y3, core), right, left, mate):
        tell(barrier, seg=target)

    tell(barrier, video=across)

    @pl.when(is_worker)
    def _():
        for target in (upper, lower):
            tell(barrier, video=target)

    lane = lax.broadcasted_iota(jnp.int32, (16, 16), 1)
    picks = [jnp.where(lane == ids_ref[0, v], 1.0, 0.0).astype(bf16) for v in range(VIDEOS)]

    def prepare(g, carry):
        span = pl.ds(pl.multiple_of(g * 384, 128), 384)
        for v in range(VIDEOS):
            bias = nn(picks[v], table[:, span])[0:1]
            part = (tok[v, :, span].astype(f32) + bias).astype(bf16)
            for i in range(4):
                xin[g * 4 + i, ROWS * v : ROWS * (v + 1), 0:96] = part[:, 96 * i : 96 * (i + 1)]
        return carry

    loads[3].wait()
    loads[4].wait()
    lax.fori_loop(0, 8, prepare, 0)
    acc[...] = jnp.zeros_like(acc)
    arrived(wall.at[me], w_sem)
    pl.semaphore_wait(barrier, jnp.where(is_worker, 9, 7))

    def y_of(k):
        return jnp.where(k == 0, y, jnp.where(k == 1, y1, jnp.where(k == 2, y2, y3)))

    def half_of(chunk, part):
        return wall.at[chunk, pl.ds(PART * part, PART)]

    def pass_on(chunk, part, target):
        block = half_of(chunk, part)
        remote(block, block, w_send, w_recv.at[chunk, part], seg=target).start()

    def start_lines(part):
        for target in (at(x, y1, core), at(x, y2, core), at(x, y3, core)):
            pass_on(me, part, target)

    start_lines(0)
    for part in range(PARTS):
        pass_on(me, part, right)
        pass_on(me, part, left)

    def landed(chunk, part):
        arrived(half_of(chunk, part), w_recv.at[chunk, part])

    def add(chunk):
        acc[...] += nn(xin[chunk, :, 0:96], wall[chunk])

    def y_step(part):
        def one(k, carry):
            chunk = at(x, y_of(k), core)
            landed(chunk, part)
            pass_on(chunk, part, right)
            pass_on(chunk, part, left)
            pass_on(chunk, part, mate)
            return carry

        one(1, 0)
        if part + 1 < PARTS:
            start_lines(part + 1)
        pass_on(me, part, mate)
        lax.fori_loop(2, 4, one, 0)

    def x_step(k, part):
        row = y_of(k)
        a = at(x + 3, row, core)
        b = at(x + 1, row, core)
        landed(a, part)
        to_right = (row + part) % 2 == 0

        @pl.when(to_right)
        def _():
            pass_on(a, part, right)

        pass_on(a, part, mate)
        landed(b, part)

        @pl.when(jnp.logical_not(to_right))
        def _():
            pass_on(b, part, left)

        pass_on(b, part, mate)

    def add_near(k, carry):
        add(at(x, y_of(k), core))
        add(at(x + 3, y_of(k), core))
        add(at(x + 1, y_of(k), core))
        return carry

    for part in range(PARTS):
        y_step(part)
        x_step(0, part)

        if part > 0:
            lax.fori_loop(1, 4, lambda k, c: (x_step(k, part - 1), c)[1], 0)
    lax.fori_loop(1, 4, lambda k, c: (x_step(k, PARTS - 1), c)[1], 0)
    lax.fori_loop(0, 4, add_near, 0)

    def other_add(chunk):
        for part in range(PARTS):
            landed(chunk, part)
        add(chunk)

    def far_step(k, carry):
        far = at(x + 2, y_of(k), core)
        for part in range(PARTS):
            landed(far, part)
            pass_on(far, part, mate)
        add(far)
        for i in (0, 1, 3):
            other_add(at(x + i, y_of(k), 1 - core))
        return carry

    lax.fori_loop(0, 4, far_step, 0)

    def last_step(k, carry):
        other_add(at(x + 2, y_of(k), 1 - core))
        return carry

    lax.fori_loop(0, 4, last_step, 0)

    low = lax.broadcasted_iota(jnp.int32, (1, 128), 1) < HS
    full = [acc[:, 128 * j : 128 * (j + 1)].astype(bf16).astype(f32) for j in range(3)]
    wanted = full[2] - full[1]
    mean_low = jnp.sum(jnp.where(low, wanted, 0.0), -1, keepdims=True) * (1.0 / HS)
    mean_high = jnp.sum(jnp.where(low, 0.0, wanted), -1, keepdims=True) * (1.0 / HS)
    full[2] = wanted - jnp.where(low, mean_low, mean_high)
    turned = [pltpu.roll(part, HS, 1) for part in full]
    for v in range(VIDEOS):
        q, k, val = [part[ROWS * v : ROWS * (v + 1)] for part in full]
        qt, kt, vt = [part[ROWS * v : ROWS * (v + 1)] for part in turned]
        for h in range(2):
            kq = jnp.where(low, k, qt) if h == 0 else jnp.where(low, kt, q)
            kq = kq.astype(bf16)
            for back in range(2):
                n = 4 * back + 2 * v + h
                order = [3, 2, 1, 0] if back else [0, 1, 2, 3]
                for t in range(4):
                    o = order[t]
                    qmsg[n, MINI * t : MINI * (t + 1)] = kq[MINI * o : MINI * (o + 1)]
                for t in range(2):
                    o, p = order[t], order[t + 2]
                    one, two = slice(MINI * o, MINI * (o + 1)), slice(MINI * p, MINI * (p + 1))
                    pair = jnp.where(low, val[one], vt[two]) if h == 0 else jnp.where(low, vt[one], val[two])
                    qmsg[n, ROWS + MINI * t : ROWS + MINI * (t + 1)] = pair.astype(bf16)

    def give(i):
        owner = jnp.where(i < 4, i, SEGS - 8 + i)

        @pl.when(owner == me)
        def _():
            pltpu.make_async_copy(qmsg.at[i], qin.at[me], q_recv.at[me]).start()

        @pl.when(owner != me)
        def _():
            remote(qmsg.at[i], qin.at[me], q_send.at[i], q_recv.at[me], seg=owner).start()

    def given(i):
        @pl.when(jnp.where(i < 4, i, SEGS - 8 + i) != me)
        def _():
            remote(qmsg.at[i], qin.at[me], q_send.at[i], q_recv.at[me], seg=right).wait_send()

    def give_soon(n, carry):
        give(jnp.where(me < 16, n, n + 4))
        return carry

    def give_later(n, carry):
        give(jnp.where(me < 16, n + 4, n))
        return carry

    def soon_given(n, carry):
        given(jnp.where(me < 16, n, n + 4))
        return carry

    def later_given(n, carry):
        given(jnp.where(me < 16, n + 4, n))
        return carry

    lax.fori_loop(0, 4, give_soon, 0)

    @pl.when(is_worker)
    def _():
        lax.fori_loop(0, 4, soon_given, 0)

    lax.fori_loop(0, 4, give_later, 0)

    loads[-1].wait()
    my_rows = pl.ds(pl.multiple_of(me * 64, 64), 64)

    def give_out_weight(i):
        target = OWN + 2 * ((i + chip) % (WORKERS // 2)) + core
        remote(ow, owall.at[my_rows], o_send, o_recv, seg=target).start()

    def piece_place(s, t):
        upper_half = jnp.where(s < 16, 0, 1)
        i = jnp.where(s < 16, 4 * s + t, 4 * (SEGS - 1 - s) + 3 - t)
        p = i % 12
        return OWN + 12 * upper_half + (p % 6) * 2 + p // 6, i // 12

    @pl.when(is_owner)
    def _():
        back = jnp.where(me < OWN, 0, 1)
        slot = jnp.where(me < OWN, me, me - (SEGS - 8))
        eta = rate_ref[head]
        loads[5].wait()
        loads[6].wait()

        def seg_of(j):
            return j + back * (SEGS - 1 - 2 * j)

        def give_answer(j, t):
            s = seg_of(j)
            target, place = piece_place(s, t + back * (3 - 2 * t))
            remote(zst.at[j, t], zbuf.at[place, slot], z_send, z_recv.at[place], seg=target).start()

        def give_across(j, t):
            target, _ = piece_place(seg_of(j), t + back * (3 - 2 * t))
            remote(zst.at[j, t], zfar.at[slot], f_send, f_recv, seg=target, video=across).start()

        tell(pair_sem, video=across)
        grads[...] = jnp.zeros_like(grads)
        row_block = lax.broadcasted_iota(jnp.int32, (ROWS, ROWS), 0) // MINI
        upto = row_block >= lax.broadcasted_iota(jnp.int32, (ROWS, ROWS), 1) // MINI

        def wait_for(j):
            s = seg_of(j)
            arrived(qin.at[s], q_recv.at[s])

        def lay_out(j, slot):
            s = seg_of(j)
            keys = qin[s, 0:ROWS, 0:HS]
            targets = jnp.concatenate([qin[s, ROWS:96, 0:HS], qin[s, ROWS:96, HS:128]], 0)
            p_turned[slot] = keys.T
            targets = targets.astype(f32)
            p_target[slot] = targets
            for t in range(4):
                p_across[slot, t] = targets[MINI * t : MINI * (t + 1)].T

        def lay_out_queries(j, slot):
            p_query[slot] = qin[seg_of(j), 0:ROWS, HS:128]

        def query_hidden(slot, keys, layer_one, grad):
            queries = p_query[slot]
            cross = jnp.where(upto, -eta * nt(queries, keys), 0.0).astype(bf16)
            return gelu_parts(nn(queries, layer_one) + nn(cross, grad))[0].astype(bf16)

        def query_answers(slot, h, j, which):
            for t in which:
                rows = slice(MINI * t, MINI * (t + 1))
                c = nt(h[rows], q_weights[slot, t])
                rho = lax.rsqrt(jnp.mean(c * c, -1, keepdims=True) + EPS)
                zst[j, t, :, 0:HS] = (p_query[slot, rows].astype(f32) + c * rho).astype(bf16)

        def answer_queries(slot, keys, layer_one, grad, j):
            query_answers(slot, query_hidden(slot, keys, layer_one, grad), j, range(4))

        def segment(j, pre, slot, begin=False, end=False):
            if not end:
                wait_for(j + 1)
            s, s_next = seg_of(j), seg_of(j if end else j + 1)
            keys = qin[s, 0:ROWS, 0:HS]
            targets = p_target[slot]
            targets_t = [p_across[slot, t] for t in range(4)]
            keys_ahead = jnp.concatenate([keys[MINI:], qin[s_next, 0:MINI, 0:HS]], 0)
            grads_before = grads[...]
            layer_one = first[...]
            if not begin:
                before = j - 1
                keys_before = qin[seg_of(before), 0:ROWS, 0:HS]
                layer_before = layer_one
                layer_one = (layer_one.astype(f32) - eta * nn(p_turned[1 - slot], grads_before)).astype(bf16)
                first[...] = layer_one
            base_k = nn(keys_ahead[:MINI], layer_one)
            cross = -eta * nt(keys_ahead, keys)
            cross_b = cross.astype(bf16)
            layer_two = second[...].astype(f32)
            mu = jnp.mean(layer_two, 0, keepdims=True)
            centred = layer_two - mu
            ahead = [base_k]
            done = []
            for t in range(4):
                rows = slice(MINI * t, MINI * (t + 1))
                h, th, x2, half = gelu_parts(pre)
                hb = h.astype(bf16)
                weights = centred.astype(bf16)
                target = targets[rows]
                c = nt(hb, weights)
                w = nn(target.astype(bf16), weights)
                u = nn(c.astype(bf16), weights)
                rho = lax.rsqrt(jnp.mean(c * c, -1, keepdims=True) + EPS)
                m = jnp.mean(target * c, -1, keepdims=True)
                r2 = rho * rho
                b = rho * (1.0 / MINI)
                a = (r2 * (1.0 / MINI)) * (EPS * r2 + rho * m)
                ct = nt(weights, hb)
                target_t = targets_t[t]
                rho_t = lax.rsqrt(jnp.sum(ct * ct, 0, keepdims=True) * (1.0 / HS) + EPS)
                m_t = jnp.sum(target_t * ct, 0, keepdims=True) * (1.0 / HS)
                r2_t = rho_t * rho_t
                b_t = rho_t * (eta / MINI)
                a_t = (r2_t * (-eta / MINI)) * (EPS * r2_t + rho_t * m_t)
                moved = centred + nn((a_t * ct + b_t * target_t).astype(bf16), hb)
                slope = gelu_slope(th, x2, half)
                grad = a * (u * slope) - b * (w * slope)
                grad_b = grad.astype(bf16)
                done.append(grad_b)
                sums = [ahead[t], None]
                for i in range(MINI):
                    col = cross[rows, MINI * t + i : MINI * t + i + 1]
                    term = jnp.broadcast_to(col, (MINI, 256)) * jnp.broadcast_to(grad[i : i + 1], (MINI, 256))
                    sums[i % 2] = term if sums[i % 2] is None else sums[i % 2] + term
                pre = sums[0] + sums[1]
                if t == 0:
                    rest = nn(keys_ahead[MINI:], layer_one)
                    ahead += [rest[MINI * i : MINI * (i + 1)] for i in range(3)]
                for r in range(t + 1, 4):
                    ahead[r] = ahead[r] + nn(cross_b[MINI * r : MINI * (r + 1), rows], grad_b)
                q_weights[slot, t] = moved.astype(bf16)
                if t == 3 and not end:
                    lay_out(j + 1, 1 - slot)
                centred = moved
                if t == 0 and not begin:
                    h_query = query_hidden(1 - slot, keys_before, layer_before, grads_before)
                if t == 0 and not begin:
                    query_answers(1 - slot, h_query, before, [0])
                if t == 1 and not begin:
                    query_answers(1 - slot, h_query, before, [1])
                if t == 2 and not begin:
                    query_answers(1 - slot, h_query, before, [2])
                if t == 3 and not begin:
                    query_answers(1 - slot, h_query, before, [3])
            grads[...] = jnp.concatenate(done, 0)
            second[...] = (centred + mu).astype(bf16)
            if not end:
                lay_out_queries(j + 1, 1 - slot)
            if not begin:
                for t in range(4):
                    give_answer(before, t)
            if end:
                for t in range(4):
                    give_across(before, t)
            return pre

        def send_out_weight(i, carry):
            give_out_weight(i)
            return carry

        lax.fori_loop(0, WORKERS // 2, send_out_weight, 0)
        wait_for(0)
        pre = nn(qin[seg_of(0), 0:MINI, 0:HS], first[...])
        lay_out(0, 0)
        lay_out_queries(0, 0)
        pre = segment(0, pre, 0, begin=True)

        def two_segments(i, pre):
            pre = segment(2 * i + 1, pre, 1)
            pre = segment(2 * i + 2, pre, 0)

            @pl.when(i == 1)
            def _():
                pl.semaphore_wait(pair_sem, 1)
                for j in range(3):
                    for t in range(4):
                        give_across(j, t)

            @pl.when(i == SEGS // 2 - 2)
            def _():
                for t in range(4):
                    give_across(SEGS - 3, t)

            return pre

        pre = lax.fori_loop(0, SEGS // 2 - 1, two_segments, pre)
        segment(SEGS - 1, pre, 1, end=True)
        s_last = seg_of(SEGS - 1)
        answer_queries(1, qin[s_last, 0:ROWS, 0:HS], first[...], grads[...], SEGS - 1)
        for t in range(4):
            give_answer(SEGS - 1, t)
            give_across(SEGS - 1, t)

    @pl.when(is_worker)
    def _():
        lax.fori_loop(0, 4, later_given, 0)

        def send_out_weight(i, carry):
            @pl.when(OWN + 2 * ((i + chip) % (WORKERS // 2)) + core != me)
            def _():
                give_out_weight(i)

            return carry

        lax.fori_loop(0, WORKERS // 2, send_out_weight, 0)
        pltpu.make_async_copy(ow, owall.at[my_rows], o_recv).start()

        for k in range(3):
            tell(ring_sem.at[k], video=upper)
            tell(ring_sem.at[k], video=lower)
            pl.semaphore_wait(ring_sem.at[k], 2)
        tell(ring_sem.at[3], video=across)
        pl.semaphore_wait(ring_sem.at[3], 1)

        upper_half = jnp.where(me < 16, 0, 1)
        r = me - OWN - 12 * upper_half
        p = r // 2 + 6 * (r % 2)
        count = jnp.where(p < 4, 6, 5)
        mine = pl.ds(pl.multiple_of(vid * 128, 128), 128)
        theirs = pl.ds(pl.multiple_of(across * 128, 128), 128)

        def place_of(n):
            place = count - 1 - n
            i = 12 * place + p
            s = jnp.where(upper_half == 0, i // 4, SEGS - 1 - i // 4)
            t = jnp.where(upper_half == 0, i % 4, 3 - i % 4)
            return place, s, t

        def spread(place, columns):
            block = heads.at[place, :, columns]

            def one(d, carry):
                remote(
                    block, block, h_send.at[place], h_recv.at[place], video=ring + (vid + d) % 8
                ).start()
                return carry

            lax.fori_loop(1, 8, one, 0)

        def write_heads(place, columns, answers):
            for v in range(VIDEOS):
                both = [answers[i].astype(f32) for i in (2 * v, 2 * v + 1, 2 * v + 4, 2 * v + 5)]
                pair = [both[h] + both[2 + h] for h in range(2)]
                heads[place, MINI * v : MINI * (v + 1), columns] = jnp.concatenate(pair, 1).astype(bf16)

        def gather_last():
            arrived(zbuf.at[0], z_recv.at[0])
            write_heads(0, mine, [zbuf[0, i, :, 0:HS] for i in range(8)])
            spread(0, mine)
            arrived(zfar, f_recv)
            write_heads(0, theirs, [zfar[i, :, 0:HS] for i in range(8)])
            spread(0, theirs)

        def gather(n):
            place, _, _ = place_of(n)
            arrived(zbuf.at[place], z_recv.at[place])
            write_heads(place, mine, [zbuf[place, i, :, 0:HS] for i in range(8)])
            block = heads.at[place, :, mine]
            remote(block, block, h_send.at[place], a_recv.at[place], video=across).start()
            spread(place, mine)

        def relay(n):
            place, _, _ = place_of(n)
            arrived(heads.at[place, :, theirs], a_recv.at[place])
            spread(place, theirs)

        def finish(n):
            place, s, t = place_of(n)
            arrived(heads.at[place, :, pl.ds(0, 128 * 14)], h_recv.at[place])
            res[place] = nn(heads[place], owall[...]).astype(bf16)

            @pl.when(s == me)
            def _():
                pltpu.make_async_copy(res.at[place], land.at[t], r_recv).start()

            @pl.when(s != me)
            def _():
                remote(res.at[place], land.at[t], r_send.at[place], r_recv, seg=s).start()

        def piece(n, carry):
            relay(n - 2)
            gather(n)

            @pl.when(n >= 4)
            def _():
                finish(n - 4)

            return carry

        half_of_all = owall.at[pl.ds(0, 1024)]
        arrived(half_of_all, o_recv)

        def share(i, carry):
            block = owall.at[pl.ds(pl.multiple_of((2 * i + core) * 64, 64), 64)]
            remote(block, block, o_send, m_recv, seg=mate).start()
            return carry

        lax.fori_loop(0, 16, share, 0)
        gather(0)
        gather(1)
        arrived(half_of_all, m_recv)
        lax.fori_loop(2, count - 1, piece, 0)
        relay(count - 3)
        finish(count - 5)
        relay(count - 2)
        finish(count - 4)
        gather_last()
        finish(count - 3)
        finish(count - 2)
        finish(count - 1)

        def piece_sent(n, carry):
            i = 12 * n + p
            s = jnp.where(upper_half == 0, i // 4, SEGS - 1 - i // 4)

            @pl.when(n == 0)
            def _():
                arrived(heads.at[n, :, pl.ds(0, 128 * 14)], h_send.at[n])

            @pl.when(n > 0)
            def _():
                arrived(heads.at[n, :, pl.ds(0, 128 * 15)], h_send.at[n])

            @pl.when(s != me)
            def _():
                remote(res.at[n], land.at[0], r_send.at[n], r_recv, seg=s).wait_send()

            return carry

        lax.fori_loop(0, count, piece_sent, 0)
        arrived(owall.at[pl.ds(0, 64 * (WORKERS // 2 - 1 + 16))], o_send)
        loads[5].wait()
        loads[6].wait()

    @pl.when(is_owner)
    def _():
        lax.fori_loop(0, 4, soon_given, 0)
        lax.fori_loop(0, 4, later_given, 0)
        arrived(owall.at[pl.ds(0, 64 * (WORKERS // 2))], o_send)
        arrived(zst, z_send)
        arrived(zst.at[pl.ds(0, 6)], f_send)

    arrived(wall.at[pl.ds(0, SEGS - 1)], w_send)

    arrived(land, r_recv)
    for t in range(4):
        for v in range(VIDEOS):
            out_ref[v, MINI * t : MINI * (t + 1)] = land[t, MINI * v : MINI * (v + 1)]


def per_device(
    tokens, prompt_ids, prompt_table, qkv_weight, out_weight, init_first, init_second, inner_rate
):
    vmem = pl.BlockSpec(memory_space=pltpu.VMEM)
    smem = pl.BlockSpec(memory_space=pltpu.SMEM)
    hbm = pl.BlockSpec(memory_space=pltpu.HBM)
    dma = pltpu.SemaphoreType.DMA
    return pl.pallas_call(
        kernel,
        out_shape=jax.ShapeDtypeStruct((VIDEOS, ROWS, 192), bf16),
        in_specs=[smem, smem] + [hbm] * 6,
        out_specs=vmem,
        scratch_shapes=[
            pltpu.VMEM((VIDEOS, ROWS, 3072), bf16),
            pltpu.VMEM((16, 3072), bf16),
            pltpu.VMEM((SEGS, VIDEOS * ROWS, 128), bf16),
            pltpu.VMEM((SEGS, 96, 384), bf16),
            pltpu.VMEM((VIDEOS * ROWS, 384), f32),
            pltpu.VMEM((8, 96, 128), bf16),
            pltpu.VMEM((SEGS, 96, 128), bf16),
            pltpu.VMEM((SEGS, 4, MINI, 128), bf16),
            pltpu.VMEM((6, 8, MINI, 128), bf16),
            pltpu.VMEM((8, MINI, 128), bf16),
            pltpu.VMEM((64, 192), bf16),
            pltpu.VMEM((2048, 192), bf16),
            pltpu.VMEM((6, VIDEOS * MINI, 2048), bf16),
            pltpu.VMEM((6, VIDEOS * MINI, 192), bf16),
            pltpu.VMEM((4, VIDEOS * MINI, 192), bf16),
            pltpu.VMEM((HS, 256), bf16),
            pltpu.VMEM((HS, 256), bf16),
            pltpu.VMEM((ROWS, 256), bf16),
            pltpu.VMEM((2, 4, HS, 256), bf16),
            pltpu.VMEM((2, ROWS, HS), bf16),
            pltpu.VMEM((2, ROWS, HS), f32),
            pltpu.VMEM((2, 4, HS, MINI), f32),
            pltpu.VMEM((2, HS, ROWS), bf16),
            dma,
            dma,
            dma,
            dma((2,)),
            dma,
            dma,
            dma((SEGS, PARTS)),
            dma((8,)),
            dma((SEGS,)),
            dma,
            dma,
            dma,
            dma,
            dma((6,)),
            dma((6,)),
            dma((6,)),
            dma((6,)),
            dma((6,)),
            dma,
            dma,
            dma,
            pltpu.SemaphoreType.REGULAR((4,)),
            pltpu.SemaphoreType.REGULAR,
        ],
        compiler_params=pltpu.CompilerParams(
            collective_id=0, has_side_effects=True, vmem_limit_bytes=60 << 20
        ),
        name="chains",
    )(
        inner_rate,
        prompt_ids.T,
        tokens,
        prompt_table,
        jnp.transpose(qkv_weight, (1, 0, 2)),
        out_weight,
        init_first,
        init_second,
    )


def solution(mesh):
    return jax.shard_map(
        per_device,
        mesh=mesh,
        in_specs=(
            P(None, "seg", None),
            P(None, "seg"),
            P(),
            P("seg", None, "video"),
            P("seg", "video"),
            P("video", None, None),
            P("video", None, None),
            P("video"),
        ),
        out_specs=P(None, "seg", "video"),
        check_vma=False,
    )
```

```python
import jax
import jax.numpy as jnp
from jax import lax
from jax.experimental import pallas as pl
from jax.experimental.pallas import tpu as pltpu
from jax.sharding import PartitionSpec as P

HS = 64
MINI = 16
SEGS = 32
GROUPS = 16
VIDEOS = 2
ROWS = 64
EPS = 1e-6
OWN = 4
WORKERS = SEGS - 2 * OWN
PARTS = 1
PART = 96 // PARTS
C0 = 0.7978845608028654
C1 = C0 * 0.044715
f32 = jnp.float32
bf16 = jnp.bfloat16


def contract(a, b, da, db):
    return lax.dot_general(a, b, (((da,), (db,)), ((), ())), preferred_element_type=f32)


def nn(a, b):
    return contract(a, b, 1, 0)


def nt(a, b):
    return contract(a, b, 1, 1)


def tn(a, b):
    return contract(a, b, 0, 0)


def gelu_parts(x):
    x2 = x * x
    t = jnp.tanh(x * (C0 + C1 * x2))
    half = 0.5 * x
    return half + half * t, t, x2, half


def gelu_slope(t, x2, half):
    return (0.5 + 0.5 * t) + half * (1.0 - t * t) * (C0 + (3.0 * C1) * x2)


def remote(src, dst, send, recv, **where):
    return pltpu.make_async_remote_copy(
        src_ref=src,
        dst_ref=dst,
        send_sem=send,
        recv_sem=recv,
        device_id=where,
        device_id_type=pl.DeviceIdType.MESH,
    )


def arrived(ref, sem):
    pltpu.make_async_copy(ref, ref, sem).wait()


def tell(sem, **where):
    pl.semaphore_signal(sem, inc=1, device_id=where, device_id_type=pl.DeviceIdType.MESH)


def kernel(
    rate_ref,
    ids_ref,
    tok_ref,
    table_ref,
    w_ref,
    ow_ref,
    first_ref,
    second_ref,
    out_ref,
    tok,
    table,
    xin,
    wall,
    acc,
    qmsg,
    qin,
    zst,
    zbuf,
    zfar,
    ow,
    owall,
    heads,
    res,
    land,
    first,
    second,
    grads,
    q_weights,
    p_query,
    p_target,
    p_across,
    p_turned,
    tok_sem,
    table_sem,
    w_sem,
    state_sem,
    ow_sem,
    w_send,
    w_recv,
    q_send,
    q_recv,
    o_send,
    o_recv,
    m_recv,
    z_send,
    z_recv,
    h_send,
    h_recv,
    a_recv,
    r_send,
    r_recv,
    f_send,
    f_recv,
    ring_sem,
    pair_sem,
):
    me = lax.axis_index("seg")
    vid = lax.axis_index("video")
    core = me % 2
    chip = me // 2
    x = chip // 4
    y = chip % 4
    is_owner = jnp.logical_or(me < OWN, me >= SEGS - OWN)
    is_worker = jnp.logical_not(is_owner)
    head = me % 2

    def at(xx, yy, cc):
        return ((xx % 4) * 4 + yy) * 2 + cc

    loads = [
        pltpu.make_async_copy(w_ref.at[j], wall.at[me, :, pl.ds(128 * j, 128)], w_sem) for j in range(3)
    ]
    loads.append(pltpu.make_async_copy(tok_ref, tok, tok_sem))
    loads.append(pltpu.make_async_copy(table_ref, table, table_sem))
    loads.append(pltpu.make_async_copy(first_ref.at[head], first, state_sem.at[0]))
    loads.append(pltpu.make_async_copy(second_ref.at[head], second, state_sem.at[1]))
    loads.append(pltpu.make_async_copy(ow_ref, ow, ow_sem))
    for load in loads:
        load.start()

    right, left, mate = at(x + 1, y, core), at(x + 3, y, core), at(x, y, 1 - core)
    y1 = y + 1 - 2 * (y % 2)
    y2 = (y + 2) % 4
    y3 = 3 - y
    ring = (vid // 8) * 8
    upper = ring + (vid + 1) % 8
    lower = ring + (vid + 7) % 8
    across = (vid + 8) % 16

    barrier = pltpu.get_barrier_semaphore()
    for target in (at(x, y1, core), at(x, y2, core), at(x, y3, core), right, left, mate):
        tell(barrier, seg=target)

    tell(barrier, video=across)

    @pl.when(is_worker)
    def _():
        for target in (upper, lower):
            tell(barrier, video=target)

    lane = lax.broadcasted_iota(jnp.int32, (16, 16), 1)
    picks = [jnp.where(lane == ids_ref[0, v], 1.0, 0.0).astype(bf16) for v in range(VIDEOS)]

    def prepare(g, carry):
        span = pl.ds(pl.multiple_of(g * 384, 128), 384)
        for v in range(VIDEOS):
            bias = nn(picks[v], table[:, span])[0:1]
            part = (tok[v, :, span].astype(f32) + bias).astype(bf16)
            for i in range(4):
                xin[g * 4 + i, ROWS * v : ROWS * (v + 1), 0:96] = part[:, 96 * i : 96 * (i + 1)]
        return carry

    loads[3].wait()
    loads[4].wait()
    lax.fori_loop(0, 8, prepare, 0)
    acc[...] = jnp.zeros_like(acc)
    arrived(wall.at[me], w_sem)
    pl.semaphore_wait(barrier, jnp.where(is_worker, 9, 7))

    def y_of(k):
        return jnp.where(k == 0, y, jnp.where(k == 1, y1, jnp.where(k == 2, y2, y3)))

    def half_of(chunk, part):
        return wall.at[chunk, pl.ds(PART * part, PART)]

    def pass_on(chunk, part, target):
        block = half_of(chunk, part)
        remote(block, block, w_send, w_recv.at[chunk, part], seg=target).start()

    def start_lines(part):
        for target in (at(x, y1, core), at(x, y2, core), at(x, y3, core)):
            pass_on(me, part, target)

    start_lines(0)
    for part in range(PARTS):
        pass_on(me, part, right)
        pass_on(me, part, left)

    def landed(chunk, part):
        arrived(half_of(chunk, part), w_recv.at[chunk, part])

    def add(chunk):
        acc[...] += nn(xin[chunk, :, 0:96], wall[chunk])

    def y_step(part):
        def one(k, carry):
            chunk = at(x, y_of(k), core)
            landed(chunk, part)
            pass_on(chunk, part, right)
            pass_on(chunk, part, left)
            pass_on(chunk, part, mate)
            return carry

        one(1, 0)
        if part + 1 < PARTS:
            start_lines(part + 1)
        pass_on(me, part, mate)
        lax.fori_loop(2, 4, one, 0)

    def x_step(k, part):
        row = y_of(k)
        a = at(x + 3, row, core)
        b = at(x + 1, row, core)
        landed(a, part)
        to_right = (row + part) % 2 == 0

        @pl.when(to_right)
        def _():
            pass_on(a, part, right)

        pass_on(a, part, mate)
        landed(b, part)

        @pl.when(jnp.logical_not(to_right))
        def _():
            pass_on(b, part, left)

        pass_on(b, part, mate)

    def add_near(k, carry):
        add(at(x, y_of(k), core))
        add(at(x + 3, y_of(k), core))
        add(at(x + 1, y_of(k), core))
        return carry

    for part in range(PARTS):
        y_step(part)
        x_step(0, part)

        if part > 0:
            lax.fori_loop(1, 4, lambda k, c: (x_step(k, part - 1), c)[1], 0)
    lax.fori_loop(1, 4, lambda k, c: (x_step(k, PARTS - 1), c)[1], 0)
    lax.fori_loop(0, 4, add_near, 0)

    def other_add(chunk):
        for part in range(PARTS):
            landed(chunk, part)
        add(chunk)

    def far_step(k, carry):
        far = at(x + 2, y_of(k), core)
        for part in range(PARTS):
            landed(far, part)
            pass_on(far, part, mate)
        return carry

    def add_rest(k, carry):
        add(at(x + 2, y_of(k), core))
        for i in (0, 1, 3):
            other_add(at(x + i, y_of(k), 1 - core))
        return carry

    lax.fori_loop(0, 4, far_step, 0)
    lax.fori_loop(0, 4, add_rest, 0)

    def last_step(k, carry):
        other_add(at(x + 2, y_of(k), 1 - core))
        return carry

    lax.fori_loop(0, 4, last_step, 0)

    low = lax.broadcasted_iota(jnp.int32, (1, 128), 1) < HS
    full = [acc[:, 128 * j : 128 * (j + 1)].astype(bf16).astype(f32) for j in range(3)]
    wanted = full[2] - full[1]
    mean_low = jnp.sum(jnp.where(low, wanted, 0.0), -1, keepdims=True) * (1.0 / HS)
    mean_high = jnp.sum(jnp.where(low, 0.0, wanted), -1, keepdims=True) * (1.0 / HS)
    full[2] = wanted - jnp.where(low, mean_low, mean_high)
    turned = [pltpu.roll(part, HS, 1) for part in full]
    for v in range(VIDEOS):
        q, k, val = [part[ROWS * v : ROWS * (v + 1)] for part in full]
        qt, kt, vt = [part[ROWS * v : ROWS * (v + 1)] for part in turned]
        for h in range(2):
            kq = jnp.where(low, k, qt) if h == 0 else jnp.where(low, kt, q)
            kq = kq.astype(bf16)
            for back in range(2):
                n = 4 * back + 2 * v + h
                order = [3, 2, 1, 0] if back else [0, 1, 2, 3]
                for t in range(4):
                    o = order[t]
                    qmsg[n, MINI * t : MINI * (t + 1)] = kq[MINI * o : MINI * (o + 1)]
                for t in range(2):
                    o, p = order[t], order[t + 2]
                    one, two = slice(MINI * o, MINI * (o + 1)), slice(MINI * p, MINI * (p + 1))
                    pair = jnp.where(low, val[one], vt[two]) if h == 0 else jnp.where(low, vt[one], val[two])
                    qmsg[n, ROWS + MINI * t : ROWS + MINI * (t + 1)] = pair.astype(bf16)

    def give(i):
        owner = jnp.where(i < 4, i, SEGS - 8 + i)

        @pl.when(owner == me)
        def _():
            pltpu.make_async_copy(qmsg.at[i], qin.at[me], q_recv.at[me]).start()

        @pl.when(owner != me)
        def _():
            remote(qmsg.at[i], qin.at[me], q_send.at[i], q_recv.at[me], seg=owner).start()

    def given(i):
        @pl.when(jnp.where(i < 4, i, SEGS - 8 + i) != me)
        def _():
            remote(qmsg.at[i], qin.at[me], q_send.at[i], q_recv.at[me], seg=right).wait_send()

    def give_soon(n, carry):
        give(jnp.where(me < 16, n, n + 4))
        return carry

    def give_later(n, carry):
        give(jnp.where(me < 16, n + 4, n))
        return carry

    def soon_given(n, carry):
        given(jnp.where(me < 16, n, n + 4))
        return carry

    def later_given(n, carry):
        given(jnp.where(me < 16, n + 4, n))
        return carry

    lax.fori_loop(0, 4, give_soon, 0)

    @pl.when(is_worker)
    def _():
        lax.fori_loop(0, 4, soon_given, 0)

    lax.fori_loop(0, 4, give_later, 0)

    loads[-1].wait()
    my_rows = pl.ds(pl.multiple_of(me * 64, 64), 64)

    def give_out_weight(i):
        target = OWN + 2 * ((i + chip) % (WORKERS // 2)) + core
        remote(ow, owall.at[my_rows], o_send, o_recv, seg=target).start()

    def piece_place(s, t):
        upper_half = jnp.where(s < 16, 0, 1)
        i = jnp.where(s < 16, 4 * s + t, 4 * (SEGS - 1 - s) + 3 - t)
        p = i % 12
        return OWN + 12 * upper_half + (p % 6) * 2 + p // 6, i // 12

    @pl.when(is_owner)
    def _():
        back = jnp.where(me < OWN, 0, 1)
        slot = jnp.where(me < OWN, me, me - (SEGS - 8))
        eta = rate_ref[head]
        loads[5].wait()
        loads[6].wait()

        def seg_of(j):
            return j + back * (SEGS - 1 - 2 * j)

        def give_answer(j, t):
            s = seg_of(j)
            target, place = piece_place(s, t + back * (3 - 2 * t))
            remote(zst.at[j, t], zbuf.at[place, slot], z_send, z_recv.at[place], seg=target).start()

        def give_across(j, t):
            target, _ = piece_place(seg_of(j), t + back * (3 - 2 * t))
            remote(zst.at[j, t], zfar.at[slot], f_send, f_recv, seg=target, video=across).start()

        tell(pair_sem, video=across)
        grads[...] = jnp.zeros_like(grads)
        row_block = lax.broadcasted_iota(jnp.int32, (ROWS, ROWS), 0) // MINI
        upto = row_block >= lax.broadcasted_iota(jnp.int32, (ROWS, ROWS), 1) // MINI

        def wait_for(j):
            s = seg_of(j)
            arrived(qin.at[s], q_recv.at[s])

        def lay_out(j, slot):
            s = seg_of(j)
            keys = qin[s, 0:ROWS, 0:HS]
            targets = jnp.concatenate([qin[s, ROWS:96, 0:HS], qin[s, ROWS:96, HS:128]], 0)
            p_turned[slot] = keys.T
            targets = targets.astype(f32)
            p_target[slot] = targets
            for t in range(4):
                p_across[slot, t] = targets[MINI * t : MINI * (t + 1)].T

        def lay_out_queries(j, slot):
            p_query[slot] = qin[seg_of(j), 0:ROWS, HS:128]

        def query_hidden(slot, keys, layer_one, grad):
            queries = p_query[slot]
            cross = jnp.where(upto, -eta * nt(queries, keys), 0.0).astype(bf16)
            return gelu_parts(nn(queries, layer_one) + nn(cross, grad))[0].astype(bf16)

        def query_answers(slot, h, j, which):
            for t in which:
                rows = slice(MINI * t, MINI * (t + 1))
                c = nt(h[rows], q_weights[slot, t])
                rho = lax.rsqrt(jnp.mean(c * c, -1, keepdims=True) + EPS)
                zst[j, t, :, 0:HS] = (p_query[slot, rows].astype(f32) + c * rho).astype(bf16)

        def answer_queries(slot, keys, layer_one, grad, j):
            query_answers(slot, query_hidden(slot, keys, layer_one, grad), j, range(4))

        def segment(j, pre, slot, begin=False, end=False):
            if not end:
                wait_for(j + 1)
            s, s_next = seg_of(j), seg_of(j if end else j + 1)
            keys = qin[s, 0:ROWS, 0:HS]
            targets = p_target[slot]
            targets_t = [p_across[slot, t] for t in range(4)]
            keys_ahead = jnp.concatenate([keys[MINI:], qin[s_next, 0:MINI, 0:HS]], 0)
            grads_before = grads[...]
            layer_one = first[...]
            if not begin:
                before = j - 1
                keys_before = qin[seg_of(before), 0:ROWS, 0:HS]
                layer_before = layer_one
                layer_one = (layer_one.astype(f32) - eta * nn(p_turned[1 - slot], grads_before)).astype(bf16)
                first[...] = layer_one
            base_k = nn(keys_ahead[:MINI], layer_one)
            cross = -eta * nt(keys_ahead, keys)
            cross_b = cross.astype(bf16)
            layer_two = second[...].astype(f32)
            mu = jnp.mean(layer_two, 0, keepdims=True)
            centred = layer_two - mu
            ahead = [base_k]
            done = []
            for t in range(4):
                rows = slice(MINI * t, MINI * (t + 1))
                h, th, x2, half = gelu_parts(pre)
                hb = h.astype(bf16)
                weights = centred.astype(bf16)
                target = targets[rows]
                c = nt(hb, weights)
                w = nn(target.astype(bf16), weights)
                u = nn(c.astype(bf16), weights)
                rho = lax.rsqrt(jnp.mean(c * c, -1, keepdims=True) + EPS)
                m = jnp.mean(target * c, -1, keepdims=True)
                r2 = rho * rho
                b = rho * (1.0 / MINI)
                a = (r2 * (1.0 / MINI)) * (EPS * r2 + rho * m)
                ct = nt(weights, hb)
                target_t = targets_t[t]
                rho_t = lax.rsqrt(jnp.sum(ct * ct, 0, keepdims=True) * (1.0 / HS) + EPS)
                m_t = jnp.sum(target_t * ct, 0, keepdims=True) * (1.0 / HS)
                r2_t = rho_t * rho_t
                b_t = rho_t * (eta / MINI)
                a_t = (r2_t * (-eta / MINI)) * (EPS * r2_t + rho_t * m_t)
                moved = centred + nn((a_t * ct + b_t * target_t).astype(bf16), hb)
                slope = gelu_slope(th, x2, half)
                grad = a * (u * slope) - b * (w * slope)
                grad_b = grad.astype(bf16)
                done.append(grad_b)
                sums = [ahead[t], None]
                for i in range(MINI):
                    col = cross[rows, MINI * t + i : MINI * t + i + 1]
                    term = jnp.broadcast_to(col, (MINI, 256)) * jnp.broadcast_to(grad[i : i + 1], (MINI, 256))
                    sums[i % 2] = term if sums[i % 2] is None else sums[i % 2] + term
                pre = sums[0] + sums[1]
                if t == 0:
                    rest = nn(keys_ahead[MINI:], layer_one)
                    ahead += [rest[MINI * i : MINI * (i + 1)] for i in range(3)]
                for r in range(t + 1, 4):
                    ahead[r] = ahead[r] + nn(cross_b[MINI * r : MINI * (r + 1), rows], grad_b)
                q_weights[slot, t] = moved.astype(bf16)
                if t == 3 and not end:
                    lay_out(j + 1, 1 - slot)
                centred = moved
                if t == 0 and not begin:
                    h_query = query_hidden(1 - slot, keys_before, layer_before, grads_before)
                if t == 0 and not begin:
                    query_answers(1 - slot, h_query, before, [0])
                if t == 1 and not begin:
                    query_answers(1 - slot, h_query, before, [1])
                if t == 2 and not begin:
                    query_answers(1 - slot, h_query, before, [2])
                if t == 3 and not begin:
                    query_answers(1 - slot, h_query, before, [3])
            grads[...] = jnp.concatenate(done, 0)
            second[...] = (centred + mu).astype(bf16)
            if not end:
                lay_out_queries(j + 1, 1 - slot)
            if not begin:
                for t in range(4):
                    give_answer(before, t)
            if end:
                for t in range(4):
                    give_across(before, t)
            return pre

        def send_out_weight(i, carry):
            give_out_weight(i)
            return carry

        lax.fori_loop(0, WORKERS // 2, send_out_weight, 0)
        wait_for(0)
        pre = nn(qin[seg_of(0), 0:MINI, 0:HS], first[...])
        lay_out(0, 0)
        lay_out_queries(0, 0)
        pre = segment(0, pre, 0, begin=True)

        def two_segments(i, pre):
            pre = segment(2 * i + 1, pre, 1)
            pre = segment(2 * i + 2, pre, 0)

            @pl.when(i == 1)
            def _():
                pl.semaphore_wait(pair_sem, 1)
                for j in range(3):
                    for t in range(4):
                        give_across(j, t)

            @pl.when(i == SEGS // 2 - 2)
            def _():
                for t in range(4):
                    give_across(SEGS - 3, t)

            return pre

        pre = lax.fori_loop(0, SEGS // 2 - 1, two_segments, pre)
        segment(SEGS - 1, pre, 1, end=True)
        s_last = seg_of(SEGS - 1)
        answer_queries(1, qin[s_last, 0:ROWS, 0:HS], first[...], grads[...], SEGS - 1)
        for t in range(4):
            give_answer(SEGS - 1, t)
            give_across(SEGS - 1, t)

    @pl.when(is_worker)
    def _():
        lax.fori_loop(0, 4, later_given, 0)

        def send_out_weight(i, carry):
            @pl.when(OWN + 2 * ((i + chip) % (WORKERS // 2)) + core != me)
            def _():
                give_out_weight(i)

            return carry

        lax.fori_loop(0, WORKERS // 2, send_out_weight, 0)
        pltpu.make_async_copy(ow, owall.at[my_rows], o_recv).start()

        for k in range(3):
            tell(ring_sem.at[k], video=upper)
            tell(ring_sem.at[k], video=lower)
            pl.semaphore_wait(ring_sem.at[k], 2)
        tell(ring_sem.at[3], video=across)
        pl.semaphore_wait(ring_sem.at[3], 1)

        upper_half = jnp.where(me < 16, 0, 1)
        r = me - OWN - 12 * upper_half
        p = r // 2 + 6 * (r % 2)
        count = jnp.where(p < 4, 6, 5)
        mine = pl.ds(pl.multiple_of(vid * 128, 128), 128)
        theirs = pl.ds(pl.multiple_of(across * 128, 128), 128)

        def place_of(n):
            place = count - 1 - n
            i = 12 * place + p
            s = jnp.where(upper_half == 0, i // 4, SEGS - 1 - i // 4)
            t = jnp.where(upper_half == 0, i % 4, 3 - i % 4)
            return place, s, t

        def spread(place, columns):
            block = heads.at[place, :, columns]

            def one(d, carry):
                remote(
                    block, block, h_send.at[place], h_recv.at[place], video=ring + (vid + d) % 8
                ).start()
                return carry

            lax.fori_loop(1, 8, one, 0)

        def write_heads(place, columns, answers):
            for v in range(VIDEOS):
                both = [answers[i].astype(f32) for i in (2 * v, 2 * v + 1, 2 * v + 4, 2 * v + 5)]
                pair = [both[h] + both[2 + h] for h in range(2)]
                heads[place, MINI * v : MINI * (v + 1), columns] = jnp.concatenate(pair, 1).astype(bf16)

        def gather_last():
            arrived(zbuf.at[0], z_recv.at[0])
            write_heads(0, mine, [zbuf[0, i, :, 0:HS] for i in range(8)])
            spread(0, mine)
            arrived(zfar, f_recv)
            write_heads(0, theirs, [zfar[i, :, 0:HS] for i in range(8)])
            spread(0, theirs)

        def gather(n):
            place, _, _ = place_of(n)
            arrived(zbuf.at[place], z_recv.at[place])
            write_heads(place, mine, [zbuf[place, i, :, 0:HS] for i in range(8)])
            block = heads.at[place, :, mine]
            remote(block, block, h_send.at[place], a_recv.at[place], video=across).start()
            spread(place, mine)

        def relay(n):
            place, _, _ = place_of(n)
            arrived(heads.at[place, :, theirs], a_recv.at[place])
            spread(place, theirs)

        def finish(n):
            place, s, t = place_of(n)
            arrived(heads.at[place, :, pl.ds(0, 128 * 14)], h_recv.at[place])
            res[place] = nn(heads[place], owall[...]).astype(bf16)

            @pl.when(s == me)
            def _():
                pltpu.make_async_copy(res.at[place], land.at[t], r_recv).start()

            @pl.when(s != me)
            def _():
                remote(res.at[place], land.at[t], r_send.at[place], r_recv, seg=s).start()

        def piece(n, carry):
            relay(n - 2)
            gather(n)

            @pl.when(n >= 4)
            def _():
                finish(n - 4)

            return carry

        half_of_all = owall.at[pl.ds(0, 1024)]
        arrived(half_of_all, o_recv)

        def share(i, carry):
            block = owall.at[pl.ds(pl.multiple_of((2 * i + core) * 64, 64), 64)]
            remote(block, block, o_send, m_recv, seg=mate).start()
            return carry

        lax.fori_loop(0, 16, share, 0)
        gather(0)
        gather(1)
        arrived(half_of_all, m_recv)
        lax.fori_loop(2, count - 1, piece, 0)
        relay(count - 3)
        finish(count - 5)
        relay(count - 2)
        finish(count - 4)
        gather_last()
        finish(count - 3)
        finish(count - 2)
        finish(count - 1)

        def piece_sent(n, carry):
            i = 12 * n + p
            s = jnp.where(upper_half == 0, i // 4, SEGS - 1 - i // 4)

            @pl.when(n == 0)
            def _():
                arrived(heads.at[n, :, pl.ds(0, 128 * 14)], h_send.at[n])

            @pl.when(n > 0)
            def _():
                arrived(heads.at[n, :, pl.ds(0, 128 * 15)], h_send.at[n])

            @pl.when(s != me)
            def _():
                remote(res.at[n], land.at[0], r_send.at[n], r_recv, seg=s).wait_send()

            return carry

        lax.fori_loop(0, count, piece_sent, 0)
        arrived(owall.at[pl.ds(0, 64 * (WORKERS // 2 - 1 + 16))], o_send)
        loads[5].wait()
        loads[6].wait()

    @pl.when(is_owner)
    def _():
        lax.fori_loop(0, 4, soon_given, 0)
        lax.fori_loop(0, 4, later_given, 0)
        arrived(owall.at[pl.ds(0, 64 * (WORKERS // 2))], o_send)
        arrived(zst, z_send)
        arrived(zst.at[pl.ds(0, 6)], f_send)

    arrived(wall.at[pl.ds(0, SEGS - 1)], w_send)

    arrived(land, r_recv)
    for t in range(4):
        for v in range(VIDEOS):
            out_ref[v, MINI * t : MINI * (t + 1)] = land[t, MINI * v : MINI * (v + 1)]


def per_device(
    tokens, prompt_ids, prompt_table, qkv_weight, out_weight, init_first, init_second, inner_rate
):
    vmem = pl.BlockSpec(memory_space=pltpu.VMEM)
    smem = pl.BlockSpec(memory_space=pltpu.SMEM)
    hbm = pl.BlockSpec(memory_space=pltpu.HBM)
    dma = pltpu.SemaphoreType.DMA
    return pl.pallas_call(
        kernel,
        out_shape=jax.ShapeDtypeStruct((VIDEOS, ROWS, 192), bf16),
        in_specs=[smem, smem] + [hbm] * 6,
        out_specs=vmem,
        scratch_shapes=[
            pltpu.VMEM((VIDEOS, ROWS, 3072), bf16),
            pltpu.VMEM((16, 3072), bf16),
            pltpu.VMEM((SEGS, VIDEOS * ROWS, 128), bf16),
            pltpu.VMEM((SEGS, 96, 384), bf16),
            pltpu.VMEM((VIDEOS * ROWS, 384), f32),
            pltpu.VMEM((8, 96, 128), bf16),
            pltpu.VMEM((SEGS, 96, 128), bf16),
            pltpu.VMEM((SEGS, 4, MINI, 128), bf16),
            pltpu.VMEM((6, 8, MINI, 128), bf16),
            pltpu.VMEM((8, MINI, 128), bf16),
            pltpu.VMEM((64, 192), bf16),
            pltpu.VMEM((2048, 192), bf16),
            pltpu.VMEM((6, VIDEOS * MINI, 2048), bf16),
            pltpu.VMEM((6, VIDEOS * MINI, 192), bf16),
            pltpu.VMEM((4, VIDEOS * MINI, 192), bf16),
            pltpu.VMEM((HS, 256), bf16),
            pltpu.VMEM((HS, 256), bf16),
            pltpu.VMEM((ROWS, 256), bf16),
            pltpu.VMEM((2, 4, HS, 256), bf16),
            pltpu.VMEM((2, ROWS, HS), bf16),
            pltpu.VMEM((2, ROWS, HS), f32),
            pltpu.VMEM((2, 4, HS, MINI), f32),
            pltpu.VMEM((2, HS, ROWS), bf16),
            dma,
            dma,
            dma,
            dma((2,)),
            dma,
            dma,
            dma((SEGS, PARTS)),
            dma((8,)),
            dma((SEGS,)),
            dma,
            dma,
            dma,
            dma,
            dma((6,)),
            dma((6,)),
            dma((6,)),
            dma((6,)),
            dma((6,)),
            dma,
            dma,
            dma,
            pltpu.SemaphoreType.REGULAR((4,)),
            pltpu.SemaphoreType.REGULAR,
        ],
        compiler_params=pltpu.CompilerParams(
            collective_id=0, has_side_effects=True, vmem_limit_bytes=60 << 20
        ),
        name="chains",
    )(
        inner_rate,
        prompt_ids.T,
        tokens,
        prompt_table,
        jnp.transpose(qkv_weight, (1, 0, 2)),
        out_weight,
        init_first,
        init_second,
    )


def solution(mesh):
    return jax.shard_map(
        per_device,
        mesh=mesh,
        in_specs=(
            P(None, "seg", None),
            P(None, "seg"),
            P(),
            P("seg", None, "video"),
            P("seg", "video"),
            P("video", None, None),
            P("video", None, None),
            P("video"),
        ),
        out_specs=P(None, "seg", "video"),
        check_vma=False,
    )
```
